256 devices in a mesh: sub: 64 (over z, y, core), grp: 4 (over x).
Axes of the slice: x: 4, y: 4, z: 8, core: 2. Of those that a mesh axis runs over, the one named last changes fastest.
Arguments:
- local_operator: float32 [64, 4, 1024, 1024], P('sub', 'grp'), as said below
- coarse_basis: float32 [64, 4, 1024, 256], P('sub', 'grp'), may hold values from -6 to 6
- neighbour_links: int32 [64, 4, 12], P('sub', 'grp'), may hold values from 0 to 1, as said below
- margin_blocks: int32 [64, 4, 14, 2], P('sub', 'grp'), may hold values from 0 to 7, as said below
Outputs:
- smoothed_basis: float32 [64, 4, 1024, 256], P('sub', 'grp')
- coupling: float32 [64, 4, 14, 256, 256], P('sub', 'grp')
The draws below stay inside these ranges and needn't reach their ends.
Inputs may be any that keep to these rules, and one draw needn't show every extreme that they name: Each local_operator block is symmetric positive definite. `neighbour_links`: entry k < 6 is 1 where subdomains (p, g) and (p + k + 1 mod 64, g) margin, entry 6 + k equals entry k of (p - k - 1 mod 64, g); entry 0 is always 1, and in every group one subdomain has all entries 1. `margin_blocks`: the two blocks of a slot differ.
All inputs are finite; a program needn't handle non-finite values.
Results may differ from the reference program's by a relative error of at most 0.0002.
Values sent between devices are 32-bit elements; how exact they have to be, the bound alone decides.
No kernel may reach another device: no remote copies, remote signals or barrier semaphores. Data moves between devices by JAX's collectives and lax.ppermute only.
A program may use at most 128 MiB of HBM per device.

```python
import math
import jax
import jax.numpy as jnp
from jax import lax

NLOC = 1024
M = 256
BLK = 128
SWEEPS = 2
OVROWS = 256
NBLK = 8
SUBS = 64
GROUPS = 4
REACH = 6
SLOTS = 14


def draw_local_operator(key, part):
    keys = jax.random.split(jax.random.fold_in(key, 7), SUBS * GROUPS)

    def single(item_key):
        key_factor, key_diagonal = jax.random.split(item_key)
        factor_entries = jax.random.normal(key_factor, (NLOC, NLOC), jnp.float32)
        diagonal_add = jnp.exp(jax.random.uniform(key_diagonal, (NLOC,), jnp.float32, math_log_low, math_log_high))
        coupled = jnp.dot(factor_entries, factor_entries.T, precision=lax.Precision.HIGHEST) / NLOC
        return coupled + jnp.diag(diagonal_add)
    return lax.map(single, keys).reshape(SUBS, GROUPS, NLOC, NLOC)


math_log_low = -0.6931472


math_log_high = 1.3862944


def draw_neighbour_links(key, part):
    key_links, key_hub = jax.random.split(jax.random.fold_in(key, 11))
    forward = jax.random.randint(key_links, (SUBS, GROUPS, REACH), 0, 2, dtype=jnp.int32)
    forward = forward.at[:, :, 0].set(1)
    hub = jax.random.randint(key_hub, (GROUPS,), 0, SUBS, dtype=jnp.int32)
    places = jnp.arange(SUBS, dtype=jnp.int32)[:, None]
    ahead_cols = []
    behind_cols = []
    for offset in range(REACH):
        forced = ((places == hub[None, :]) | ((places + offset + 1) % SUBS == hub[None, :])).astype(jnp.int32)
        column = jnp.maximum(forward[:, :, offset], forced)
        ahead_cols.append(column)
        behind_cols.append(jnp.roll(column, offset + 1, axis=0))
    return jnp.stack(ahead_cols + behind_cols, axis=2)


def draw_margin_blocks(key, part):
    key_first, key_step = jax.random.split(jax.random.fold_in(key, 23))
    first = jax.random.randint(key_first, (SUBS, GROUPS, SLOTS), 0, NBLK, dtype=jnp.int32)
    stride = jax.random.randint(key_step, (SUBS, GROUPS, SLOTS), 1, NBLK, dtype=jnp.int32)
    return jnp.stack([first, (first + stride) % NBLK], axis=-1)


def level_of(key, dims, cuts, smallest, largest):
    loudness = 1.0
    for position, parts in cuts:
        steps = jax.random.uniform(jax.random.fold_in(jax.random.fold_in(key, 6), position), (parts,), jnp.float32, smallest / len(cuts), largest / len(cuts))
        loudness = loudness * jnp.repeat(jnp.exp(steps), dims[position] // parts).reshape((-1,) + (1,) * (len(dims) - 1 - position))
    return loudness


def bell_draw(rng, extent, width, reach, cuts=(), held_as=jnp.bfloat16):
    level = level_of(rng, extent, cuts, -0.22, 0.18) if cuts else 1.0
    result = jax.random.normal(rng, extent, jnp.float32) * width * level
    return jnp.minimum(jnp.maximum(result, -reach), reach).astype(held_as)


def setup_inputs(seed: int = 0) -> dict:
    splits = jax.random.split(jax.random.key(seed), 5)
    local_operator = draw_local_operator(jax.random.fold_in(splits[4], 71), 0)
    coarse_basis = bell_draw(splits[1], (SUBS, GROUPS, NLOC, M), 1.0, 6.0, ((0, 64), (1, 4)), jnp.float32)
    neighbour_links = draw_neighbour_links(jax.random.fold_in(splits[4], 71), 0)
    margin_blocks = draw_margin_blocks(jax.random.fold_in(splits[4], 71), 0)
    return dict(local_operator=local_operator, coarse_basis=coarse_basis, neighbour_links=neighbour_links, margin_blocks=margin_blocks)


damping = 0.5
highest = lax.Precision.HIGHEST

def partner(slot_index, reach_sub):
    if slot_index < reach_sub:
        return slot_index + reach_sub
    if slot_index < 2 * reach_sub:
        return slot_index - reach_sub
    if slot_index == 2 * reach_sub:
        return slot_index + 1
    return slot_index - 1

def neighbour(stacked, slot_index, reach_sub):
    if slot_index < reach_sub:
        return jnp.roll(stacked, -(slot_index + 1), axis=0)
    if slot_index < 2 * reach_sub:
        return jnp.roll(stacked, slot_index - reach_sub + 1, axis=0)
    if slot_index == 2 * reach_sub:
        return jnp.roll(stacked, -1, axis=1)
    return jnp.roll(stacked, 1, axis=1)

def products(local_operator, current):

    def single(operands):
        return jnp.dot(operands[0].astype(jnp.float32), operands[1].astype(jnp.float32), precision=highest, preferred_element_type=jnp.float32)
    flattened = lax.map(single, (local_operator.reshape(-1, NLOC, NLOC), current.reshape(-1, NLOC, M)))
    return flattened.reshape(SUBS, GROUPS, NLOC, M)

def reference(local_operator, coarse_basis, neighbour_links, margin_blocks):
    selector = (margin_blocks[..., None] == jnp.arange(NBLK, dtype=jnp.int32)).astype(jnp.float32)
    active = jnp.concatenate([neighbour_links.astype(jnp.float32), jnp.ones((SUBS, GROUPS, 2), jnp.float32)], axis=2)
    diagonal = jnp.diagonal(local_operator, axis1=2, axis2=3)[..., None]

    def margin(stacked, slot_index):
        blocked = stacked.reshape(SUBS, GROUPS, NBLK, BLK, M)
        picked = jnp.einsum('pgjb,pgbrm->pgjrm', selector[:, :, slot_index], blocked, precision=highest)
        return picked.reshape(SUBS, GROUPS, OVROWS, M) * active[:, :, slot_index, None, None]

    def assemble(current):
        product = products(local_operator, current)
        assembled = product.reshape(SUBS, GROUPS, NBLK, BLK, M)
        for slot_index in range(SLOTS):
            received = neighbour(margin(product, partner(slot_index, REACH)), slot_index, REACH)
            assembled = assembled + jnp.einsum('pgjb,pgjrm->pgbrm', selector[:, :, slot_index], received.reshape(SUBS, GROUPS, 2, BLK, M), precision=highest)
        return assembled.reshape(SUBS, GROUPS, NLOC, M)
    current = coarse_basis
    for sweep_index in range(SWEEPS):
        current = current - damping * assemble(current) / diagonal
    product = products(local_operator, current)
    gram_block = jnp.einsum('pgim,pgin->pgmn', current, product, precision=highest)
    factor = jnp.linalg.cholesky(gram_block)
    identity = jnp.broadcast_to(jnp.eye(M, dtype=jnp.float32), factor.shape)
    inverse = lax.linalg.triangular_solve(factor, identity, left_side=True, lower=True)
    pieces = []
    for slot_index in range(SLOTS):
        own_rows = margin(current, slot_index)
        far_rows = neighbour(margin(product, partner(slot_index, REACH)), slot_index, REACH)
        galerkin = jnp.einsum('pgrm,pgrn->pgmn', own_rows, far_rows, precision=highest)
        half_scaled = jnp.einsum('pgam,pgmn->pgan', inverse, galerkin, precision=highest)
        far_inverse = neighbour(inverse, slot_index, REACH)
        pieces.append(math.sqrt(NLOC) * jnp.einsum('pgan,pgbn->pgab', half_scaled, far_inverse, precision=highest))
    return (current, jnp.stack(pieces, axis=2))
```

```python
import functools
import math

import jax
import jax.numpy as jnp
from jax import lax
from jax.experimental import pallas as pl
from jax.experimental.pallas import tpu as pltpu
from jax.sharding import PartitionSpec as P

BLK = 128
REACH = 6
SLOTS = 2 * REACH + 2
RING = 4
WORDS = 3 * SLOTS
OTHER = WORDS
SOURCE = 2 * WORDS
CORE = 3 * WORDS
WRAPS = CORE + 1
F32 = jnp.float32
BF16 = jnp.bfloat16


def sign(i):
    return 1 - 2 * (i % 2)


def along_ring(i, step):
    core, y, z = i % 2, (i // 2) % RING, i // (2 * RING)
    return (z * RING + (y + step) % RING) * 2 + core


def wraps(i):
    y = (i // 2) % RING
    return y == (0 if i % 2 == 0 else RING - 1)


def route_ring(i):
    return along_ring(i, sign(i))


def route_source(i):
    return along_ring(i, -sign(i))


def route_near(i):
    return i - 2 * sign(i)


def route_far(i):
    return i + 6 * sign(i)


def route_ahead(i):
    return route_source(i) + 4 * sign(i)


def route_back(i):
    return route_source(i) - 4 * sign(i)


def route_layer(i):
    return route_source(i) + (2 if wraps(i) else -6) * sign(i)


def route_core(i):
    return i ^ 1


def send(block, route):
    n = lax.axis_size("sub")
    return lax.ppermute(block, "sub", [(i, route(i) % n) for i in range(n)])


def send_group(block, distance):
    n = lax.axis_size("grp")
    return lax.ppermute(block, "grp", [(i, (i + distance) % n) for i in range(n)])


def slot_of(step, core):
    up = step - 1 if step > 0 else REACH - 1 - step
    down = REACH - 1 + step if step > 0 else -step - 1
    return jnp.where(core == 0, up, down)


def rows_of(tab, base, slot, j):
    return pl.ds(pl.multiple_of(tab[base + 2 * slot + j] * BLK, BLK), BLK)


def flag_of(tab, base, slot):
    return tab[base + 2 * SLOTS + slot].astype(F32)


def pick(tab, base, slot, source, target, place):
    for j in range(2):
        target[pl.ds((2 * place + j) * BLK, BLK), :] = source[rows_of(tab, base, slot, j), :]


def halves(x):
    high = x.astype(BF16)
    return high, (x - high.astype(F32)).astype(BF16)


def dot(a, b, dims=((1,), (0,))):
    return lax.dot_general(a, b, (dims, ((), ())), preferred_element_type=F32)


def dot_full(a, b, dims=((1,), (0,))):
    return lax.dot_general(
        a, b, (dims, ((), ())), precision=lax.Precision.HIGHEST, preferred_element_type=F32
    )


def dot_split(a, b, dims=((1,), (0,))):
    a_high, a_low = halves(a)
    b_high, b_low = halves(b)
    return dot(a_high, b_high, dims) + dot(a_high, b_low, dims) + dot(a_low, b_high, dims)


def apply_operator(high, low, x, out):
    x_high, x_low = halves(x)
    width = x.shape[1]
    both = jnp.concatenate([x_high, x_low], axis=1)
    step = 256
    for r in range(0, high.shape[0], step):
        first = dot(high[r : r + step, :], both)
        out[r : r + step, :] = (
            first[:, :width] + first[:, width:] + dot(low[r : r + step, :], x_high)
        )


def pack(tab, core, full, near, far, up, down):
    pick(tab, 0, slot_of(-2, core), full, near, 0)
    pick(tab, 0, slot_of(-1, core), full, near, 1)
    pick(tab, 0, slot_of(6, core), full, far, 0)
    pick(tab, 0, 2 * REACH, full, up, 0)
    pick(tab, 0, 2 * REACH + 1, full, down, 0)


def start_kernel(tab, a, x, high, low, scale, full, near, far, up, down):
    core = tab[CORE]
    n = a.shape[0]
    eye = (
        lax.broadcasted_iota(jnp.int32, (BLK, BLK), 0)
        == lax.broadcasted_iota(jnp.int32, (BLK, BLK), 1)
    )
    for r in range(0, n, BLK):
        rows = a[r : r + BLK, :]
        row_high, row_low = halves(rows)
        high[r : r + BLK, :] = row_high
        low[r : r + BLK, :] = row_low
        square = rows[:, r : r + BLK]
        diagonal = jnp.sum(jnp.where(eye, square, 0.0), axis=1, keepdims=True)
        scale[r : r + BLK, :] = jnp.broadcast_to(0.5 / diagonal, (BLK, BLK))
    apply_operator(high, low, x[:, :BLK], full)
    pack(tab, core, full, near, far, up, down)


def next_kernel(tab, high, low, x, full, near, far, up, down):
    apply_operator(high, low, x[:, BLK:], full)
    pack(tab, tab[CORE], full, near, far, up, down)


def relay_kernel(tab, ring, ahead, back, layer):
    core, wrapped = tab[CORE], tab[WRAPS]
    pick(tab, SOURCE, slot_of(4, core), ring, ahead, 0)
    pick(tab, SOURCE, slot_of(5, core), ring, ahead, 1)
    pick(tab, SOURCE, slot_of(-4, core), ring, back, 0)
    pick(tab, SOURCE, slot_of(-3, core), ring, back, 1)
    mine = jnp.where(wrapped == 1, slot_of(2, core), slot_of(-6, core))
    theirs = jnp.where(wrapped == 1, slot_of(3, core), slot_of(-5, core))
    pick(tab, SOURCE, mine, ring, layer, 0)
    pick(tab, SOURCE, theirs, ring, layer, 1)


def add_rows(tab, base, slot, total, part):
    flag = flag_of(tab, base, slot)
    for j in range(2):
        rows = rows_of(tab, base, slot, j)
        total[rows, :] += flag * part(j)


def packet(ref, place):
    return lambda j: ref[pl.ds((2 * place + j) * BLK, BLK), :]


def block_rows(tab, base, slot, ref):
    return lambda j: ref[rows_of(tab, base, slot, j), :]


def cross_sum_kernel(tab, full, ring, near, ahead, back, layer, total):
    core, wrapped = tab[CORE], tab[WRAPS]
    other = 1 - core
    total[...] = jnp.zeros(total.shape, F32)
    add = functools.partial(add_rows, tab, OTHER)
    add(slot_of(1, other), total, block_rows(tab, 0, slot_of(1, core), full))
    add(slot_of(-1, other), total, packet(near, 1))
    here = jnp.where(wrapped == 1, slot_of(-5, core), slot_of(3, core))
    at = jnp.where(wrapped == 1, slot_of(-5, other), slot_of(3, other))
    add(at, total, block_rows(tab, SOURCE, here, ring))
    at = jnp.where(wrapped == 1, slot_of(3, other), slot_of(-5, other))
    add(at, total, packet(layer, 1))
    add(slot_of(5, other), total, packet(ahead, 1))
    add(slot_of(-3, other), total, packet(back, 1))


def cross_copy_kernel(tab, full, ring, near, ahead, back, layer, out):
    core, wrapped = tab[CORE], tab[WRAPS]
    half = 2 * BLK
    pick(tab, 0, slot_of(1, core), full, out, 0)
    out[half : 2 * half, :] = near[half:, :]
    here = jnp.where(wrapped == 1, slot_of(-5, core), slot_of(3, core))
    for j in range(2):
        local = ring[rows_of(tab, SOURCE, here, j), :]
        far = layer[half + j * BLK : half + (j + 1) * BLK, :]
        at = 2 * half + j * BLK
        out[at : at + BLK, :] = jnp.where(wrapped == 1, far, local)
        out[at + half : at + half + BLK, :] = jnp.where(wrapped == 1, local, far)
    out[4 * half : 5 * half, :] = ahead[half:, :]
    out[5 * half : 6 * half, :] = back[half:, :]


def gather_sum(tab, total, full, ring, near, far, ahead, back, layer, above, below, cross):
    core, wrapped = tab[CORE], tab[WRAPS]
    total[...] = full[...] + cross[...]
    add = functools.partial(add_rows, tab, 0)
    add(slot_of(2, core), total, packet(near, 0))
    add(slot_of(-6, core), total, packet(far, 0))
    here = jnp.where(wrapped == 1, slot_of(-6, core), slot_of(2, core))
    at = jnp.where(wrapped == 1, slot_of(6, core), slot_of(-2, core))
    add(at, total, block_rows(tab, SOURCE, here, ring))
    at = jnp.where(wrapped == 1, slot_of(-2, core), slot_of(6, core))
    add(at, total, packet(layer, 0))
    add(slot_of(-4, core), total, packet(ahead, 0))
    add(slot_of(4, core), total, packet(back, 0))
    add(2 * REACH, total, packet(above, 0))
    add(2 * REACH + 1, total, packet(below, 0))


def inverse_factor(gram_ref):
    tile = 8
    count = BLK // tile
    row_id = lax.broadcasted_iota(jnp.int32, (tile, BLK), 0)
    lane_id = lax.broadcasted_iota(jnp.int32, (tile, BLK), 1)
    g = [gram_ref[tile * i : tile * i + tile, :] for i in range(count)]
    w = [jnp.where(lane_id == row_id + tile * i, 1.0, 0.0).astype(F32) for i in range(count)]
    for b in range(count):
        scales = jnp.ones((tile, BLK), F32)
        for r in range(tile):
            k = tile * b + r
            row = g[b][r : r + 1, :]
            pivot = jnp.broadcast_to(row[:, k : k + 1], (1, BLK))
            recip = 1.0 / pivot
            scales = jnp.where(row_id == r, jnp.broadcast_to(lax.rsqrt(pivot), (tile, BLK)), scales)
            g_row = jnp.broadcast_to(row * recip, (tile, BLK))
            w_row = jnp.broadcast_to(w[b][r : r + 1, :] * recip, (tile, BLK))
            for i in range(b, count):
                if i == b and r == tile - 1:
                    continue
                column = jnp.broadcast_to(g[i][:, k : k + 1], (tile, BLK))
                if i == b:
                    column = jnp.where(row_id > r, column, 0.0)
                g[i] = g[i] - column * g_row
                w[i] = w[i] - column * w_row
        w[b] = w[b] * scales
    return jnp.concatenate(w, axis=0)


def sweep_kernel(tab, high, low, scale, x, *refs):
    received, outs, total = refs[:10], refs[10:16], refs[16]
    x_new, full, near, far, up, down = outs
    gather_sum(tab, total, *received)
    half = x_new.shape[1]
    offset = x.shape[1] - half
    column = refs[17]
    x_new[...] = x[:, column * half : (column + 1) * half] - total[...] * scale[...] if offset else (
        x[...] - total[...] * scale[...]
    )
    apply_operator(high, low, x_new[...], full)
    pack(tab, tab[CORE], full, near, far, up, down)


def sweep_kernel_at(column, tab, high, low, scale, x, *refs):
    sweep_kernel(tab, high, low, scale, x, *refs, column)


def symmetric(g):
    return 0.5 * (g + g.T)


ROWS = ((0,), (0,))
LANES = ((1,), (1,))


def first_factor_kernel(tab, high, low, scale, x, *refs):
    received, outs, (total, gram) = refs[:10], refs[10:19], refs[19:]
    x_new, product, inverse, scaled, basis, near, far, up, down = outs
    gather_sum(tab, total, *received)
    x_new[...] = x[...] - total[...] * scale[...]
    apply_operator(high, low, x_new[...], product)
    gram[...] = symmetric(dot_full(x_new[...], product[...], ROWS))
    inverse[...] = inverse_factor(gram)
    scaled[...] = dot_split(product[...], inverse[...], LANES)
    basis[...] = dot_split(x_new[...], inverse[...], LANES)
    pack(tab, tab[CORE], scaled, near, far, up, down)


def second_factor_kernel(tab, high, low, scale, x, *refs):
    received = refs[:10]
    x0, product0, inverse0, scaled0, basis0 = refs[10:15]
    x_out, scaled, basis_high, basis_low, near, far, up, down = refs[15:23]
    total, gram, product, inverse = refs[23:]
    gather_sum(tab, total, *received)
    x_new = x[...] - total[...] * scale[...]
    x_out[:, :BLK] = x0[...]
    x_out[:, BLK:] = x_new
    apply_operator(high, low, x_new, product)
    corner = 0.5 * (
        dot_full(x_new, product0[...], ROWS) + dot_full(product[...], x0[...], ROWS)
    )
    lower = dot_full(corner, inverse0[...], LANES)
    gram[...] = symmetric(dot_full(x_new, product[...], ROWS)) - dot_full(lower, lower, LANES)
    inverse[...] = inverse_factor(gram)
    rest = product[...] - dot_split(scaled0[...], lower, LANES)
    scaled[...] = dot_split(rest, inverse[...], LANES)
    pack(tab, tab[CORE], scaled, near, far, up, down)
    rest = x_new - dot_split(basis0[...], lower, LANES)
    basis1 = dot_split(rest, inverse[...], LANES)
    factor = math.sqrt(x.shape[0])
    for b in range(x.shape[0] // BLK):
        for h, part in enumerate((basis0[b * BLK : (b + 1) * BLK, :], basis1[b * BLK : (b + 1) * BLK])):
            block_high, block_low = halves(factor * part.T)
            basis_high[b, h * BLK : (h + 1) * BLK, :] = block_high
            basis_low[b, h * BLK : (h + 1) * BLK, :] = block_low


def coupling_kernel(tab, basis_high, basis_low, *refs):
    received = (refs[:9], refs[9:18])
    out, stage, sem = refs[18:]
    core, wrapped = tab[CORE], tab[WRAPS]
    half = 2 * BLK
    local = jnp.where(wrapped == 1, slot_of(-6, core), slot_of(2, core))

    def couple(place, slot, part):
        flag = flag_of(tab, 0, slot)
        for h in range(2):
            value = jnp.zeros((half, BLK), F32)
            for j in range(2):
                b = tab[2 * slot + j]
                left_high, left_low = basis_high[b], basis_low[b]
                right_high, right_low = halves(part(received[h], j))
                both = jnp.concatenate([right_high, right_low], axis=1)
                first = dot(left_high, both)
                value += first[:, :BLK] + first[:, BLK:] + dot(left_low, right_high)
            stage[place, :, h * BLK : (h + 1) * BLK] = flag * value
        pltpu.make_async_copy(stage.at[place], out.at[slot], sem.at[place]).start()

    def at(index, place):
        return lambda refs, j: refs[index][(2 * place + j) * BLK : (2 * place + j + 1) * BLK, :]

    def from_ring(refs, j):
        return refs[0][rows_of(tab, SOURCE, local, j), :]

    slots = [
        (2 * REACH, at(6, 0)),
        (2 * REACH + 1, at(7, 0)),
        (slot_of(2, core), at(1, 0)),
        (slot_of(-6, core), at(2, 0)),
        (jnp.where(wrapped == 1, slot_of(6, core), slot_of(-2, core)), from_ring),
        (jnp.where(wrapped == 1, slot_of(-2, core), slot_of(6, core)), at(5, 0)),
        (slot_of(-4, core), at(3, 0)),
        (slot_of(4, core), at(4, 0)),
    ]
    for place, step in enumerate((1, -1, 3, -5, 5, -3)):
        slots.append((slot_of(step, core), at(8, place)))
    for place, (slot, part) in enumerate(slots):
        couple(place, slot, part)
    for place, (slot, part) in enumerate(slots):
        pltpu.make_async_copy(stage.at[place], out.at[slot], sem.at[place]).wait()


VMEM = pl.BlockSpec(memory_space=pltpu.VMEM)
SMEM = pl.BlockSpec(memory_space=pltpu.SMEM)
ANY = pl.BlockSpec(memory_space=pl.ANY)


def f32(*shape):
    return jax.ShapeDtypeStruct(shape, F32)


def b16(*shape):
    return jax.ShapeDtypeStruct(shape, BF16)


def call(kernel, outs, *args, scratch=(), out_specs=None, flops=0):
    moved = sum(math.prod(a.shape) * a.dtype.itemsize for a in (*args, *outs))
    return pl.pallas_call(
        kernel,
        out_shape=tuple(outs),
        in_specs=[SMEM] + [VMEM] * (len(args) - 1),
        out_specs=tuple(out_specs or [VMEM] * len(outs)),
        scratch_shapes=list(scratch),
        compiler_params=pltpu.CompilerParams(vmem_limit_bytes=24 * 2**20),
        cost_estimate=pl.CostEstimate(flops=flops, bytes_accessed=moved, transcendentals=0),
    )(*args)


def on_device(local_operator, coarse_basis, neighbour_links, margin_blocks):
    matrix = local_operator[0, 0]
    initial = coarse_basis[0, 0]
    n, columns = initial.shape
    width = BLK
    assert columns == 2 * width
    own = jnp.concatenate(
        [
            margin_blocks.reshape(2 * SLOTS),
            neighbour_links.reshape(2 * REACH),
            jnp.ones((2,), jnp.int32),
        ]
    )
    other = send(own, route_core)
    source = send(own, route_ring)
    place = lax.axis_index("sub")
    core = place % 2
    y = (place // 2) % RING
    wrapped = (y == jnp.where(core == 0, 0, RING - 1)).astype(jnp.int32)
    where = jnp.stack([core, wrapped])
    blank = jnp.zeros((2 * WORDS,), jnp.int32)
    own_tab = jnp.concatenate([own, blank, where])
    tab = jnp.concatenate([own, other, source, where])

    full, pair, one = f32(n, width), f32(4 * BLK, width), f32(2 * BLK, width)
    packed = [pair, one, one, one]
    acc = pltpu.VMEM((n, width), F32)
    square = pltpu.VMEM((BLK, BLK), F32)
    product_flops = 6 * n * n * width

    def depart(block, near, far, up, down):
        return [
            send(block, route_ring),
            send(near, route_near),
            send(far, route_far),
            send_group(down, -1),
            send_group(up, 1),
        ]

    def arrive(block, first, cross):
        ring, near, far, above, below = first
        ahead, back, layer = call(relay_kernel, [pair, pair, pair], tab, ring)
        ahead = send(ahead, route_ahead)
        back = send(back, route_back)
        layer = send(layer, route_layer)
        kernel, out = cross
        (theirs,) = call(kernel, [out], tab, block, ring, near, ahead, back, layer)
        theirs = send(theirs, route_core)
        return [ring, near, far, ahead, back, layer, above, below, theirs]

    total = (cross_sum_kernel, full)
    copies = (cross_copy_kernel, f32(12 * BLK, width))

    high, low, scale, *sent0 = call(
        start_kernel,
        [b16(n, n), b16(n, n), f32(n, width), full, *packed],
        own_tab,
        matrix,
        initial,
        flops=product_flops,
    )
    first0 = depart(*sent0)
    sent1 = call(next_kernel, [full, *packed], own_tab, high, low, initial, flops=product_flops)
    first1 = depart(*sent1)

    def sweep(column, x, block, received):
        return call(
            functools.partial(sweep_kernel_at, column),
            [full, full, *packed],
            tab,
            high,
            low,
            scale,
            x,
            block,
            *received,
            scratch=[acc],
            flops=product_flops,
        )

    x0, *sent0_next = sweep(0, initial, sent0[0], arrive(sent0[0], first0, total))
    first0 = depart(*sent0_next)
    x1, *sent1_next = sweep(1, initial, sent1[0], arrive(sent1[0], first1, total))
    first1 = depart(*sent1_next)

    x0, product0, inverse0, scaled0, basis0, *sent0 = call(
        first_factor_kernel,
        [full, full, f32(BLK, BLK), full, full, *packed],
        tab,
        high,
        low,
        scale,
        x0,
        sent0_next[0],
        *arrive(sent0_next[0], first0, total),
        scratch=[acc, square],
        flops=2 * product_flops,
    )
    first0 = depart(scaled0, *sent0)
    smoothed, scaled1, basis_high, basis_low, *sent1 = call(
        second_factor_kernel,
        [f32(n, columns), full, b16(n // BLK, columns, BLK), b16(n // BLK, columns, BLK), *packed],
        tab,
        high,
        low,
        scale,
        x1,
        sent1_next[0],
        *arrive(sent1_next[0], first1, total),
        x0,
        product0,
        inverse0,
        scaled0,
        basis0,
        scratch=[acc, square, acc, square],
        flops=2 * product_flops,
    )
    first1 = depart(scaled1, *sent1)
    received0 = arrive(scaled0, first0, copies)
    received1 = arrive(scaled1, first1, copies)
    (coupling,) = call(
        coupling_kernel,
        [f32(SLOTS, columns, columns)],
        tab,
        basis_high,
        basis_low,
        *received0,
        *received1,
        scratch=[
            pltpu.VMEM((SLOTS, columns, columns), F32),
            pltpu.SemaphoreType.DMA((SLOTS,)),
        ],
        out_specs=[ANY],
        flops=6 * SLOTS * columns**3,
    )
    return (smoothed[None, None], coupling[None, None])


def solution(mesh):
    in_specs = (
        P("sub", "grp", None, None),
        P("sub", "grp", None, None),
        P("sub", "grp", None),
        P("sub", "grp", None, None),
    )
    out_specs = (P("sub", "grp", None, None), P("sub", "grp", None, None, None))
    return jax.shard_map(
        on_device, mesh=mesh, in_specs=in_specs, out_specs=out_specs, check_vma=False
    )
```

```python
import functools
import math

import jax
import jax.numpy as jnp
from jax import lax
from jax.experimental import pallas as pl
from jax.experimental.pallas import tpu as pltpu
from jax.sharding import PartitionSpec as P

BLK = 128
REACH = 6
SLOTS = 2 * REACH + 2
RING = 4
WORDS = 3 * SLOTS
OTHER = WORDS
SOURCE = 2 * WORDS
CORE = 3 * WORDS
WRAPS = CORE + 1
F32 = jnp.float32
BF16 = jnp.bfloat16


def sign(i):
    return 1 - 2 * (i % 2)


def along_ring(i, step):
    core, y, z = i % 2, (i // 2) % RING, i // (2 * RING)
    return (z * RING + (y + step) % RING) * 2 + core


def wraps(i):
    y = (i // 2) % RING
    return y == (0 if i % 2 == 0 else RING - 1)


def route_ring(i):
    return along_ring(i, sign(i))


def route_source(i):
    return along_ring(i, -sign(i))


def route_near(i):
    return i - 2 * sign(i)


def route_far(i):
    return i + 6 * sign(i)


def route_ahead(i):
    return route_source(i) + 4 * sign(i)


def route_back(i):
    return route_source(i) - 4 * sign(i)


def route_layer(i):
    return route_source(i) + (2 if wraps(i) else -6) * sign(i)


def route_core(i):
    return i ^ 1


def send(block, route):
    n = lax.axis_size("sub")
    return lax.ppermute(block, "sub", [(i, route(i) % n) for i in range(n)])


def send_group(block, distance):
    n = lax.axis_size("grp")
    return lax.ppermute(block, "grp", [(i, (i + distance) % n) for i in range(n)])


def slot_of(step, core):
    up = step - 1 if step > 0 else REACH - 1 - step
    down = REACH - 1 + step if step > 0 else -step - 1
    return jnp.where(core == 0, up, down)


def rows_of(tab, base, slot, j):
    return pl.ds(pl.multiple_of(tab[base + 2 * slot + j] * BLK, BLK), BLK)


def flag_of(tab, base, slot):
    return tab[base + 2 * SLOTS + slot].astype(F32)


def pick(tab, base, slot, source, target, place):
    for j in range(2):
        target[pl.ds((2 * place + j) * BLK, BLK), :] = source[rows_of(tab, base, slot, j), :]


def halves(x):
    high = x.astype(BF16)
    return high, (x - high.astype(F32)).astype(BF16)


def dot(a, b, dims=((1,), (0,))):
    return lax.dot_general(a, b, (dims, ((), ())), preferred_element_type=F32)


def dot_full(a, b, dims=((1,), (0,))):
    return lax.dot_general(
        a, b, (dims, ((), ())), precision=lax.Precision.HIGHEST, preferred_element_type=F32
    )


def dot_split(a, b, dims=((1,), (0,))):
    a_high, a_low = halves(a)
    b_high, b_low = halves(b)
    return dot(a_high, b_high, dims) + dot(a_high, b_low, dims) + dot(a_low, b_high, dims)


def apply_operator(high, low, x, out):
    x_high, x_low = halves(x)
    width = x.shape[1]
    both = jnp.concatenate([x_high, x_low], axis=1)
    step = 256
    for r in range(0, high.shape[0], step):
        first = dot(high[r : r + step, :], both)
        out[r : r + step, :] = (
            first[:, :width] + first[:, width:] + dot(low[r : r + step, :], x_high)
        )


def pack(tab, core, full, near, far, up, down):
    pick(tab, 0, slot_of(-2, core), full, near, 0)
    pick(tab, 0, slot_of(-1, core), full, near, 1)
    pick(tab, 0, slot_of(6, core), full, far, 0)
    pick(tab, 0, 2 * REACH, full, up, 0)
    pick(tab, 0, 2 * REACH + 1, full, down, 0)


def start_kernel(tab, a, x, high, low, scale, full, near, far, up, down):
    core = tab[CORE]
    n = a.shape[0]
    eye = (
        lax.broadcasted_iota(jnp.int32, (BLK, BLK), 0)
        == lax.broadcasted_iota(jnp.int32, (BLK, BLK), 1)
    )
    for r in range(0, n, BLK):
        rows = a[r : r + BLK, :]
        row_high, row_low = halves(rows)
        high[r : r + BLK, :] = row_high
        low[r : r + BLK, :] = row_low
        square = rows[:, r : r + BLK]
        diagonal = jnp.sum(jnp.where(eye, square, 0.0), axis=1, keepdims=True)
        scale[r : r + BLK, :] = jnp.broadcast_to(0.5 / diagonal, (BLK, BLK))
    apply_operator(high, low, x[:, :BLK], full)
    pack(tab, core, full, near, far, up, down)


def next_kernel(tab, high, low, x, full, near, far, up, down):
    apply_operator(high, low, x[:, BLK:], full)
    pack(tab, tab[CORE], full, near, far, up, down)


def relay_kernel(tab, ring, ahead, back, layer):
    core, wrapped = tab[CORE], tab[WRAPS]
    pick(tab, SOURCE, slot_of(4, core), ring, ahead, 0)
    pick(tab, SOURCE, slot_of(5, core), ring, ahead, 1)
    pick(tab, SOURCE, slot_of(-4, core), ring, back, 0)
    pick(tab, SOURCE, slot_of(-3, core), ring, back, 1)
    mine = jnp.where(wrapped == 1, slot_of(2, core), slot_of(-6, core))
    theirs = jnp.where(wrapped == 1, slot_of(3, core), slot_of(-5, core))
    pick(tab, SOURCE, mine, ring, layer, 0)
    pick(tab, SOURCE, theirs, ring, layer, 1)


def add_rows(tab, base, slot, total, part):
    flag = flag_of(tab, base, slot)
    for j in range(2):
        rows = rows_of(tab, base, slot, j)
        total[rows, :] += flag * part(j)


def packet(ref, place):
    return lambda j: ref[pl.ds((2 * place + j) * BLK, BLK), :]


def block_rows(tab, base, slot, ref):
    return lambda j: ref[rows_of(tab, base, slot, j), :]


def cross_sum_kernel(tab, full, ring, near, far, ahead, back, layer, above, below, total, mine):
    core, wrapped = tab[CORE], tab[WRAPS]
    other = 1 - core
    total[...] = jnp.zeros(total.shape, F32)
    add = functools.partial(add_rows, tab, OTHER)
    add(slot_of(1, other), total, block_rows(tab, 0, slot_of(1, core), full))
    add(slot_of(-1, other), total, packet(near, 1))
    here = jnp.where(wrapped == 1, slot_of(-5, core), slot_of(3, core))
    at = jnp.where(wrapped == 1, slot_of(-5, other), slot_of(3, other))
    add(at, total, block_rows(tab, SOURCE, here, ring))
    at = jnp.where(wrapped == 1, slot_of(3, other), slot_of(-5, other))
    add(at, total, packet(layer, 1))
    add(slot_of(5, other), total, packet(ahead, 1))
    add(slot_of(-3, other), total, packet(back, 1))
    mine[...] = full[...]
    add = functools.partial(add_rows, tab, 0)
    add(slot_of(2, core), mine, packet(near, 0))
    add(slot_of(-6, core), mine, packet(far, 0))
    here = jnp.where(wrapped == 1, slot_of(-6, core), slot_of(2, core))
    at = jnp.where(wrapped == 1, slot_of(6, core), slot_of(-2, core))
    add(at, mine, block_rows(tab, SOURCE, here, ring))
    at = jnp.where(wrapped == 1, slot_of(-2, core), slot_of(6, core))
    add(at, mine, packet(layer, 0))
    add(slot_of(-4, core), mine, packet(ahead, 0))
    add(slot_of(4, core), mine, packet(back, 0))
    add(2 * REACH, mine, packet(above, 0))
    add(2 * REACH + 1, mine, packet(below, 0))


def cross_copy_kernel(tab, full, ring, near, far, ahead, back, layer, above, below, out):
    core, wrapped = tab[CORE], tab[WRAPS]
    half = 2 * BLK
    pick(tab, 0, slot_of(1, core), full, out, 0)
    out[half : 2 * half, :] = near[half:, :]
    here = jnp.where(wrapped == 1, slot_of(-5, core), slot_of(3, core))
    for j in range(2):
        local = ring[rows_of(tab, SOURCE, here, j), :]
        far = layer[half + j * BLK : half + (j + 1) * BLK, :]
        at = 2 * half + j * BLK
        out[at : at + BLK, :] = jnp.where(wrapped == 1, far, local)
        out[at + half : at + half + BLK, :] = jnp.where(wrapped == 1, local, far)
    out[4 * half : 5 * half, :] = ahead[half:, :]
    out[5 * half : 6 * half, :] = back[half:, :]


def inverse_factor(gram):
    tile = 8
    count = BLK // tile
    row_id = lax.broadcasted_iota(jnp.int32, (tile, BLK), 0)
    lane_id = lax.broadcasted_iota(jnp.int32, (tile, BLK), 1)
    eye = (
        lax.broadcasted_iota(jnp.int32, (BLK, BLK), 0)
        == lax.broadcasted_iota(jnp.int32, (BLK, BLK), 1)
    )
    diagonal = jnp.where(eye, gram, 0.0)
    left = lax.rsqrt(jnp.sum(diagonal, axis=1, keepdims=True))
    top = lax.rsqrt(jnp.sum(diagonal, axis=0, keepdims=True))
    unit = gram * left * top
    g = [unit[tile * i : tile * i + tile, :] for i in range(count)]
    w = [jnp.where(lane_id == row_id + tile * i, 1.0, 0.0).astype(F32) for i in range(count)]

    def spread(v):
        return jnp.broadcast_to(v, (tile, BLK))

    def entry(row, k):
        return jnp.broadcast_to(row[:, k : k + 1], (1, BLK))

    for b in range(count):
        scales = jnp.ones((tile, BLK), F32)
        for r in range(0, tile, 2):
            k = tile * b + r
            row0, row1 = g[b][r : r + 1, :], g[b][r + 1 : r + 2, :]
            a00, a01, a11 = entry(row0, k), entry(row0, k + 1), entry(row1, k + 1)
            det = a00 * a11 - a01 * a01
            inv00, inv_det = 1.0 / a00, 1.0 / det
            p00, p01, p11 = a11 * inv_det, -a01 * inv_det, a00 * inv_det
            g0, g1 = spread(p00 * row0 + p01 * row1), spread(p01 * row0 + p11 * row1)
            w0, w1 = w[b][r : r + 1, :], w[b][r + 1 : r + 2, :]
            u0, u1 = spread(p00 * w0 + p01 * w1), spread(p01 * w0 + p11 * w1)
            scales = jnp.where(row_id == r, spread(lax.rsqrt(a00)), scales)
            scales = jnp.where(row_id == r + 1, spread(lax.rsqrt(det * inv00)), scales)
            w[b] = jnp.where(row_id == r + 1, spread(w1 - (a01 * inv00) * w0), w[b])
            for i in range(b, count):
                if i == b and r == tile - 2:
                    continue
                c0, c1 = spread(g[i][:, k : k + 1]), spread(g[i][:, k + 1 : k + 2])
                if i == b:
                    c0 = jnp.where(row_id > r + 1, c0, 0.0)
                    c1 = jnp.where(row_id > r + 1, c1, 0.0)
                g[i] = g[i] - c0 * g0 - c1 * g1
                w[i] = w[i] - c0 * u0 - c1 * u1
        w[b] = w[b] * scales
    return jnp.concatenate(w, axis=0) * top


def sweep_kernel(column, tab, high, low, scale, x, mine, cross, *outs):
    x_new, full, near, far, up, down = outs
    change = (mine[...] + cross[...]) * scale[...]
    x_new[...] = x[:, column * BLK : (column + 1) * BLK] - change
    apply_operator(high, low, x_new[...], full)
    pack(tab, tab[CORE], full, near, far, up, down)


def symmetric(g):
    return 0.5 * (g + g.T)


ROWS = ((0,), (0,))
LANES = ((1,), (1,))


def first_factor_kernel(tab, high, low, scale, x, mine, cross, *outs):
    x_new, product, inverse, scaled, basis, near, far, up, down = outs
    x_new[...] = x[...] - (mine[...] + cross[...]) * scale[...]
    apply_operator(high, low, x_new[...], product)
    gram = symmetric(dot_full(x_new[...], product[...], ROWS))
    inverse[...] = inverse_factor(gram)
    scaled[...] = dot_split(product[...], inverse[...], LANES)
    pack(tab, tab[CORE], scaled, near, far, up, down)
    basis[...] = dot_split(x_new[...], inverse[...], LANES)


def second_product_kernel(
    high, low, scale, x, mine, cross, x0, product0, inverse0, x_out, product, lower, rest
):
    x_new = x[...] - (mine[...] + cross[...]) * scale[...]
    x_out[:, :BLK] = x0[...]
    x_out[:, BLK:] = x_new
    apply_operator(high, low, x_new, product)
    corner = 0.5 * (
        dot_full(x_new, product0[...], ROWS) + dot_full(product[...], x0[...], ROWS)
    )
    side = dot_full(corner, inverse0[...], LANES)
    lower[...] = side
    gram = symmetric(dot_full(x_new, product[...], ROWS))
    rest[...] = gram - dot_full(side, side, LANES)


def second_factor_kernel(
    tab, product, lower, rest, scaled0, inverse, scaled, near, far, up, down
):
    inverse[...] = inverse_factor(rest[...])
    change = product[...] - dot_split(scaled0[...], lower[...], LANES)
    scaled[...] = dot_split(change, inverse[...], LANES)
    pack(tab, tab[CORE], scaled, near, far, up, down)


def basis_kernel(x, lower, basis0, inverse, basis_high, basis_low):
    change = x[:, BLK:] - dot_split(basis0[...], lower[...], LANES)
    basis1 = dot_split(change, inverse[...], LANES)
    factor = math.sqrt(x.shape[0])
    for b in range(x.shape[0] // BLK):
        rows = slice(b * BLK, (b + 1) * BLK)
        for h, part in enumerate((basis0[rows, :], basis1[rows, :])):
            block_high, block_low = halves(factor * part.T)
            basis_high[b, h * BLK : (h + 1) * BLK, :] = block_high
            basis_low[b, h * BLK : (h + 1) * BLK, :] = block_low


def coupling_kernel(tab, basis_high, basis_low, *refs):
    received = (refs[:9], refs[9:18])
    out, stage, sem = refs[18:]
    core, wrapped = tab[CORE], tab[WRAPS]
    half = 2 * BLK
    local = jnp.where(wrapped == 1, slot_of(-6, core), slot_of(2, core))

    def couple(place, slot, part):
        flag = flag_of(tab, 0, slot)
        for h in range(2):
            value = jnp.zeros((half, BLK), F32)
            for j in range(2):
                b = tab[2 * slot + j]
                left_high, left_low = basis_high[b], basis_low[b]
                right_high, right_low = halves(part(received[h], j))
                both = jnp.concatenate([right_high, right_low], axis=1)
                first = dot(left_high, both)
                value += first[:, :BLK] + first[:, BLK:] + dot(left_low, right_high)
            stage[place, :, h * BLK : (h + 1) * BLK] = flag * value
        pltpu.make_async_copy(stage.at[place], out.at[slot], sem.at[place]).start()

    def at(index, place):
        return lambda refs, j: refs[index][(2 * place + j) * BLK : (2 * place + j + 1) * BLK, :]

    def from_ring(refs, j):
        return refs[0][rows_of(tab, SOURCE, local, j), :]

    slots = [
        (2 * REACH, at(6, 0)),
        (2 * REACH + 1, at(7, 0)),
        (slot_of(2, core), at(1, 0)),
        (slot_of(-6, core), at(2, 0)),
        (jnp.where(wrapped == 1, slot_of(6, core), slot_of(-2, core)), from_ring),
        (jnp.where(wrapped == 1, slot_of(-2, core), slot_of(6, core)), at(5, 0)),
        (slot_of(-4, core), at(3, 0)),
        (slot_of(4, core), at(4, 0)),
    ]
    for place, step in enumerate((1, -1, 3, -5, 5, -3)):
        slots.append((slot_of(step, core), at(8, place)))
    for place, (slot, part) in enumerate(slots):
        couple(place, slot, part)
    for place, (slot, part) in enumerate(slots):
        pltpu.make_async_copy(stage.at[place], out.at[slot], sem.at[place]).wait()


VMEM = pl.BlockSpec(memory_space=pltpu.VMEM)
SMEM = pl.BlockSpec(memory_space=pltpu.SMEM)
ANY = pl.BlockSpec(memory_space=pl.ANY)


def f32(*shape):
    return jax.ShapeDtypeStruct(shape, F32)


def b16(*shape):
    return jax.ShapeDtypeStruct(shape, BF16)


def call(kernel, outs, *args, scratch=(), out_specs=None, table=True):
    return pl.pallas_call(
        kernel,
        out_shape=tuple(outs),
        in_specs=[SMEM if table else VMEM] + [VMEM] * (len(args) - 1),
        out_specs=tuple(out_specs or [VMEM] * len(outs)),
        scratch_shapes=list(scratch),
        compiler_params=pltpu.CompilerParams(vmem_limit_bytes=16 * 2**20),
        cost_estimate=pl.CostEstimate(flops=1, bytes_accessed=1, transcendentals=0),
    )(*args)


def on_device(local_operator, coarse_basis, neighbour_links, margin_blocks):
    matrix = local_operator[0, 0]
    initial = coarse_basis[0, 0]
    n, columns = initial.shape
    width = BLK
    assert columns == 2 * width
    own = jnp.concatenate(
        [
            margin_blocks.reshape(2 * SLOTS),
            neighbour_links.reshape(2 * REACH),
            jnp.ones((2,), jnp.int32),
        ]
    )
    other = send(own, route_core)
    source = send(own, route_ring)
    place = lax.axis_index("sub")
    core = place % 2
    y = (place // 2) % RING
    wrapped = (y == jnp.where(core == 0, 0, RING - 1)).astype(jnp.int32)
    tab = jnp.concatenate([own, other, source, jnp.stack([core, wrapped])])

    full, pair, one = f32(n, width), f32(4 * BLK, width), f32(2 * BLK, width)
    square = f32(width, width)
    packed = [pair, one, one, one]

    def depart(block, near, far, up, down):
        return [
            send(block, route_ring),
            send(near, route_near),
            send(far, route_far),
            send_group(down, -1),
            send_group(up, 1),
        ]

    def arrive(block, first, cross, outs):
        ring, near, far, above, below = first
        ahead, back, layer = call(relay_kernel, [pair, pair, pair], tab, ring)
        ahead = send(ahead, route_ahead)
        back = send(back, route_back)
        layer = send(layer, route_layer)
        parts = [ring, near, far, ahead, back, layer, above, below]
        theirs, *rest = call(cross, outs, tab, block, *parts)
        return parts, rest, send(theirs, route_core)

    def summed(block, first):
        _, (mine,), theirs = arrive(block, first, cross_sum_kernel, [full, full])
        return mine, theirs

    def copied(block, first):
        parts, _, theirs = arrive(block, first, cross_copy_kernel, [f32(12 * BLK, width)])
        return parts + [theirs]

    high, low, scale, *sent0 = call(
        start_kernel, [b16(n, n), b16(n, n), full, full, *packed], tab, matrix, initial
    )
    first0 = depart(*sent0)
    sent1 = call(next_kernel, [full, *packed], tab, high, low, initial)
    first1 = depart(*sent1)

    def sweep(column, block, first):
        return call(
            functools.partial(sweep_kernel, column),
            [full, full, *packed],
            tab,
            high,
            low,
            scale,
            initial,
            *summed(block, first),
        )

    x0, *sent0 = sweep(0, sent0[0], first0)
    first0 = depart(*sent0)
    x1, *sent1 = sweep(1, sent1[0], first1)
    first1 = depart(*sent1)

    x0, product0, inverse0, scaled0, basis0, *packets0 = call(
        first_factor_kernel,
        [full, full, square, full, full, *packed],
        tab,
        high,
        low,
        scale,
        x0,
        *summed(sent0[0], first0),
    )
    first0 = depart(scaled0, *packets0)
    smoothed, product1, lower, rest = call(
        second_product_kernel,
        [f32(n, columns), full, square, square],
        high,
        low,
        scale,
        x1,
        *summed(sent1[0], first1),
        x0,
        product0,
        inverse0,
        table=False,
    )
    inverse1, scaled1, *packets1 = call(
        second_factor_kernel,
        [square, full, *packed],
        tab,
        product1,
        lower,
        rest,
        scaled0,
    )
    first1 = depart(scaled1, *packets1)
    turned = b16(n // BLK, columns, BLK)
    basis = call(
        basis_kernel, [turned, turned], smoothed, lower, basis0, inverse1, table=False
    )
    received0 = copied(scaled0, first0)
    received1 = copied(scaled1, first1)
    (coupling,) = call(
        coupling_kernel,
        [f32(SLOTS, columns, columns)],
        tab,
        *basis,
        *received0,
        *received1,
        scratch=[
            pltpu.VMEM((SLOTS, columns, columns), F32),
            pltpu.SemaphoreType.DMA((SLOTS,)),
        ],
        out_specs=[ANY],
    )
    return (smoothed[None, None], coupling[None, None])


def solution(mesh):
    in_specs = (
        P("sub", "grp", None, None),
        P("sub", "grp", None, None),
        P("sub", "grp", None),
        P("sub", "grp", None, None),
    )
    out_specs = (P("sub", "grp", None, None), P("sub", "grp", None, None, None))
    return jax.shard_map(
        on_device, mesh=mesh, in_specs=in_specs, out_specs=out_specs, check_vma=False
    )
```

```python
import functools
import math

import jax
import jax.numpy as jnp
from jax import lax
from jax.experimental import pallas as pl
from jax.experimental.pallas import tpu as pltpu
from jax.sharding import PartitionSpec as P

BLK = 128
REACH = 6
SLOTS = 2 * REACH + 2
RING = 4
OWN, OTHER, SOURCE = range(3)
CORE = 3 * SLOTS
WRAPS = CORE + 1
F32 = jnp.float32
BF16 = jnp.bfloat16


def sign(i):
    return 1 - 2 * (i % 2)


def along_ring(i, step):
    core, y, z = i % 2, (i // 2) % RING, i // (2 * RING)
    return (z * RING + (y + step) % RING) * 2 + core


def wraps(i):
    y = (i // 2) % RING
    return y == (0 if i % 2 == 0 else RING - 1)


def route_ring(i):
    return along_ring(i, sign(i))


def route_source(i):
    return along_ring(i, -sign(i))


def route_near(i):
    return i - 2 * sign(i)


def route_far(i):
    return i + 6 * sign(i)


def route_ahead(i):
    return route_source(i) + 4 * sign(i)


def route_back(i):
    return route_source(i) - 4 * sign(i)


def route_layer(i):
    return route_source(i) + (2 if wraps(i) else -6) * sign(i)


def route_core(i):
    return i ^ 1


def send(block, route):
    n = lax.axis_size("sub")
    return lax.ppermute(block, "sub", [(i, route(i) % n) for i in range(n)])


def send_group(block, distance):
    n = lax.axis_size("grp")
    return lax.ppermute(block, "grp", [(i, (i + distance) % n) for i in range(n)])


def slot_of(step, core):
    up = step - 1 if step > 0 else REACH - 1 - step
    down = REACH - 1 + step if step > 0 else -step - 1
    return jnp.where(core == 0, up, down)


def rows_of(tab, base, slot, j):
    return pl.ds(pl.multiple_of(tab[base][2 * slot + j] * BLK, BLK), BLK)


def flag_of(tab, base, slot):
    return tab[base][2 * SLOTS + slot].astype(F32)


def pick(tab, base, slot, source, target, place):
    for j in range(2):
        target[pl.ds((2 * place + j) * BLK, BLK), :] = source[rows_of(tab, base, slot, j), :]


def halves(x):
    high = x.astype(BF16)
    return high, (x - high.astype(F32)).astype(BF16)


def dot(a, b, dims=((1,), (0,))):
    return lax.dot_general(a, b, (dims, ((), ())), preferred_element_type=F32)


def dot_full(a, b, dims=((1,), (0,))):
    return lax.dot_general(
        a, b, (dims, ((), ())), precision=lax.Precision.HIGHEST, preferred_element_type=F32
    )


def dot_split(a, b, dims=((1,), (0,))):
    a_high, a_low = halves(a)
    b_high, b_low = halves(b)
    return dot(a_high, b_high, dims) + dot(a_high, b_low, dims) + dot(a_low, b_high, dims)


def apply_operator(high, low, x, out):
    x_high, x_low = halves(x)
    width = x.shape[1]
    both = jnp.concatenate([x_high, x_low], axis=1)
    step = 256
    for r in range(0, high.shape[0], step):
        first = dot(high[r : r + step, :], both)
        out[r : r + step, :] = (
            first[:, :width] + first[:, width:] + dot(low[r : r + step, :], x_high)
        )


def pack(tab, core, full, near, far, up, down):
    pick(tab, OWN, slot_of(-2, core), full, near, 0)
    pick(tab, OWN, slot_of(-1, core), full, near, 1)
    pick(tab, OWN, slot_of(6, core), full, far, 0)
    pick(tab, OWN, 2 * REACH, full, up, 0)
    pick(tab, OWN, 2 * REACH + 1, full, down, 0)


def start_kernel(a, x, high, low, scale, full):
    n = a.shape[0]
    step = 2 * BLK
    x_high, x_low = halves(x[:, :BLK])
    both = jnp.concatenate([x_high, x_low], axis=1)
    eye = (
        lax.broadcasted_iota(jnp.int32, (BLK, BLK), 0)
        == lax.broadcasted_iota(jnp.int32, (BLK, BLK), 1)
    )
    for r in range(0, n, step):
        row_high, row_low = halves(a[r : r + step, :])
        high[r : r + step, :] = row_high
        low[r : r + step, :] = row_low
        first = dot(row_high, both)
        full[r : r + step, :] = first[:, :BLK] + first[:, BLK:] + dot(row_low, x_high)
        for d in range(r, r + step, BLK):
            square = a[d : d + BLK, d : d + BLK]
            diagonal = jnp.sum(jnp.where(eye, square, 0.0), axis=1, keepdims=True)
            scale[d : d + BLK, :] = jnp.broadcast_to(0.5 / diagonal, (BLK, BLK))


def next_kernel(tab, high, low, x, first, full, *packets):
    core = tab[OWN][CORE]
    pack(tab, core, first, *packets[:4])
    apply_operator(high, low, x[:, BLK:], full)
    pack(tab, core, full, *packets[4:])


def relay_kernel(tab, ring, ahead, back, layer):
    core, wrapped = tab[OWN][CORE], tab[OWN][WRAPS]
    pick(tab, SOURCE, slot_of(4, core), ring, ahead, 0)
    pick(tab, SOURCE, slot_of(5, core), ring, ahead, 1)
    pick(tab, SOURCE, slot_of(-4, core), ring, back, 0)
    pick(tab, SOURCE, slot_of(-3, core), ring, back, 1)
    mine = jnp.where(wrapped == 1, slot_of(2, core), slot_of(-6, core))
    theirs = jnp.where(wrapped == 1, slot_of(3, core), slot_of(-5, core))
    pick(tab, SOURCE, mine, ring, layer, 0)
    pick(tab, SOURCE, theirs, ring, layer, 1)


def add_rows(tab, base, slot, total, part):
    flag = flag_of(tab, base, slot)
    for j in range(2):
        rows = rows_of(tab, base, slot, j)
        total[rows, :] += flag * part(j)


def packet(ref, place):
    return lambda j: ref[pl.ds((2 * place + j) * BLK, BLK), :]


def block_rows(tab, base, slot, ref):
    return lambda j: ref[rows_of(tab, base, slot, j), :]


def cross_sum_kernel(tab, full, ring, near, far, ahead, back, layer, above, below, total, mine):
    core, wrapped = tab[OWN][CORE], tab[OWN][WRAPS]
    other = 1 - core
    total[...] = jnp.zeros(total.shape, F32)
    add = functools.partial(add_rows, tab, OTHER)
    add(slot_of(1, other), total, block_rows(tab, OWN, slot_of(1, core), full))
    add(slot_of(-1, other), total, packet(near, 1))
    here = jnp.where(wrapped == 1, slot_of(-5, core), slot_of(3, core))
    at = jnp.where(wrapped == 1, slot_of(-5, other), slot_of(3, other))
    add(at, total, block_rows(tab, SOURCE, here, ring))
    at = jnp.where(wrapped == 1, slot_of(3, other), slot_of(-5, other))
    add(at, total, packet(layer, 1))
    add(slot_of(5, other), total, packet(ahead, 1))
    add(slot_of(-3, other), total, packet(back, 1))
    mine[...] = full[...]
    add = functools.partial(add_rows, tab, OWN)
    add(slot_of(2, core), mine, packet(near, 0))
    add(slot_of(-6, core), mine, packet(far, 0))
    here = jnp.where(wrapped == 1, slot_of(-6, core), slot_of(2, core))
    at = jnp.where(wrapped == 1, slot_of(6, core), slot_of(-2, core))
    add(at, mine, block_rows(tab, SOURCE, here, ring))
    at = jnp.where(wrapped == 1, slot_of(-2, core), slot_of(6, core))
    add(at, mine, packet(layer, 0))
    add(slot_of(-4, core), mine, packet(ahead, 0))
    add(slot_of(4, core), mine, packet(back, 0))
    add(2 * REACH, mine, packet(above, 0))
    add(2 * REACH + 1, mine, packet(below, 0))


def cross_copy_kernel(tab, full, ring, near, far, ahead, back, layer, above, below, out):
    core, wrapped = tab[OWN][CORE], tab[OWN][WRAPS]
    half = 2 * BLK
    pick(tab, OWN, slot_of(1, core), full, out, 0)
    out[half : 2 * half, :] = near[half:, :]
    here = jnp.where(wrapped == 1, slot_of(-5, core), slot_of(3, core))
    for j in range(2):
        local = ring[rows_of(tab, SOURCE, here, j), :]
        far = layer[half + j * BLK : half + (j + 1) * BLK, :]
        at = 2 * half + j * BLK
        out[at : at + BLK, :] = jnp.where(wrapped == 1, far, local)
        out[at + half : at + half + BLK, :] = jnp.where(wrapped == 1, local, far)
    out[4 * half : 5 * half, :] = ahead[half:, :]
    out[5 * half : 6 * half, :] = back[half:, :]


def inverse_factor(gram):
    tile = 8
    count = BLK // tile
    row_id = lax.broadcasted_iota(jnp.int32, (tile, BLK), 0)
    lane_id = lax.broadcasted_iota(jnp.int32, (tile, BLK), 1)
    eye = (
        lax.broadcasted_iota(jnp.int32, (BLK, BLK), 0)
        == lax.broadcasted_iota(jnp.int32, (BLK, BLK), 1)
    )
    diagonal = jnp.where(eye, gram, 0.0)
    left = lax.rsqrt(jnp.sum(diagonal, axis=1, keepdims=True))
    top = lax.rsqrt(jnp.sum(diagonal, axis=0, keepdims=True))
    unit = gram * left * top
    g = [unit[tile * i : tile * i + tile, :] for i in range(count)]
    w = [jnp.where(lane_id == row_id + tile * i, 1.0, 0.0).astype(F32) for i in range(count)]

    def columns(t, base):
        return [jnp.broadcast_to(t[:, base + q : base + q + 1], (tile, BLK)) for q in range(tile)]

    def row(t, r):
        return jnp.broadcast_to(t[r : r + 1, :], (tile, BLK))

    def total(terms):
        while len(terms) > 1:
            terms = [terms[j] + terms[j + 1] for j in range(0, len(terms), 2)]
        return terms[0]

    for b in range(count):
        cols = columns(g[b], tile * b)
        pg, pw = g[b], w[b]
        inv = jnp.ones((tile, BLK), F32)
        for q in range(0, tile, 2):
            c0, c1 = cols[q], cols[q + 1]
            a00, a01, a11 = row(c0, q), row(c1, q), row(c1, q + 1)
            inv0 = 1.0 / a00
            inv_det = 1.0 / (a00 * a11 - a01 * a01)
            inv = jnp.where(row_id == q, inv0, jnp.where(row_id == q + 1, a00 * inv_det, inv))
            below = row_id > q + 1
            step0 = jnp.where(
                below, (c0 * a11 - c1 * a01) * inv_det, jnp.where(row_id == q + 1, a01 * inv0, 0.0)
            )
            step1 = jnp.where(below, (c1 * a00 - c0 * a01) * inv_det, 0.0)

            def reduce(t):
                return t - step0 * row(t, q) - step1 * row(t, q + 1)

            for m in range(q + 1, tile):
                cols[m] = reduce(cols[m])
            pg, pw = reduce(pg), reduce(pw)
        w[b] = pw * jnp.sqrt(inv)
        if b == count - 1:
            break
        zg, zw = pg * inv, pw * inv
        for q in range(tile - 1, 0, -1):
            back = jnp.where(row_id < q, cols[q] * inv, 0.0)
            zg, zw = zg - back * row(zg, q), zw - back * row(zw, q)
        rows_g = [row(zg, q) for q in range(tile)]
        rows_w = [row(zw, q) for q in range(tile)]
        for i in range(b + 1, count):
            cs = columns(g[i], tile * b)
            g[i] = g[i] - total([c * z for c, z in zip(cs, rows_g)])
            w[i] = w[i] - total([c * z for c, z in zip(cs, rows_w)])
    return jnp.concatenate(w, axis=0) * top


def sweep_kernel(column, tab, high, low, scale, x, mine, cross, *outs):
    x_new, full, near, far, up, down = outs
    change = (mine[...] + cross[...]) * scale[...]
    x_new[...] = x[:, column * BLK : (column + 1) * BLK] - change
    apply_operator(high, low, x_new[...], full)
    pack(tab, tab[OWN][CORE], full, near, far, up, down)


def symmetric(g):
    return 0.5 * (g + g.T)


ROWS = ((0,), (0,))
LANES = ((1,), (1,))


def first_factor_kernel(tab, high, low, scale, x, mine, cross, *outs):
    x_new, product, inverse, scaled, near, far, up, down = outs
    x_new[...] = x[...] - (mine[...] + cross[...]) * scale[...]
    apply_operator(high, low, x_new[...], product)
    gram = symmetric(dot_full(x_new[...], product[...], ROWS))
    inverse[...] = inverse_factor(gram)
    scaled[...] = dot_split(product[...], inverse[...], LANES)
    pack(tab, tab[OWN][CORE], scaled, near, far, up, down)


def second_product_kernel(
    high, low, scale, x, mine, cross, x0, product0, inverse0, x_out, product, lower, rest
):
    x_new = x[...] - (mine[...] + cross[...]) * scale[...]
    x_out[:, :BLK] = x0[...]
    x_out[:, BLK:] = x_new
    apply_operator(high, low, x_new, product)
    corner = 0.5 * (
        dot_full(x_new, product0[...], ROWS) + dot_full(product[...], x0[...], ROWS)
    )
    side = dot_full(corner, inverse0[...], LANES)
    lower[...] = side
    gram = symmetric(dot_full(x_new, product[...], ROWS))
    rest[...] = gram - dot_full(side, side, LANES)


def second_factor_kernel(
    tab, product, lower, rest, scaled0, inverse, scaled, near, far, up, down
):
    inverse[...] = inverse_factor(rest[...])
    change = product[...] - dot_split(scaled0[...], lower[...], LANES)
    scaled[...] = dot_split(change, inverse[...], LANES)
    pack(tab, tab[OWN][CORE], scaled, near, far, up, down)


def basis_kernel(x, lower, inverse0, inverse, basis_high, basis_low):
    basis0 = dot_split(x[:, :BLK], inverse0[...], LANES)
    change = x[:, BLK:] - dot_split(basis0, lower[...], LANES)
    basis1 = dot_split(change, inverse[...], LANES)
    factor = math.sqrt(x.shape[0])
    for b in range(x.shape[0] // BLK):
        rows = slice(b * BLK, (b + 1) * BLK)
        for h, part in enumerate((basis0[rows], basis1[rows])):
            block_high, block_low = halves(factor * part.T)
            basis_high[b, h * BLK : (h + 1) * BLK, :] = block_high
            basis_low[b, h * BLK : (h + 1) * BLK, :] = block_low


def coupling_kernel(tab, basis_high, basis_low, *refs):
    received = (refs[:9], refs[9:18])
    out, stage, sem = refs[18:]
    core, wrapped = tab[OWN][CORE], tab[OWN][WRAPS]
    local = jnp.where(wrapped == 1, slot_of(-6, core), slot_of(2, core))

    def couple(place, slot, part):
        flag = flag_of(tab, OWN, slot)
        first, second = tab[OWN][2 * slot], tab[OWN][2 * slot + 1]
        left_high = jnp.concatenate([basis_high[first], basis_high[second]], axis=1)
        left_low = jnp.concatenate([basis_low[first], basis_low[second]], axis=1)
        for h in range(2):
            right = jnp.concatenate([part(received[h], 0), part(received[h], 1)], axis=0)
            right_high, right_low = halves(right)
            both = jnp.concatenate([right_high, right_low], axis=1)
            whole = dot(left_high, both)
            value = whole[:, :BLK] + whole[:, BLK:] + dot(left_low, right_high)
            stage[place, :, h * BLK : (h + 1) * BLK] = flag * value
        pltpu.make_async_copy(stage.at[place], out.at[slot], sem.at[place]).start()

    def at(index, place):
        return lambda refs, j: refs[index][(2 * place + j) * BLK : (2 * place + j + 1) * BLK, :]

    def from_ring(refs, j):
        return refs[0][rows_of(tab, SOURCE, local, j), :]

    slots = [
        (2 * REACH, at(6, 0)),
        (2 * REACH + 1, at(7, 0)),
        (slot_of(2, core), at(1, 0)),
        (slot_of(-6, core), at(2, 0)),
        (jnp.where(wrapped == 1, slot_of(6, core), slot_of(-2, core)), from_ring),
        (jnp.where(wrapped == 1, slot_of(-2, core), slot_of(6, core)), at(5, 0)),
        (slot_of(-4, core), at(3, 0)),
        (slot_of(4, core), at(4, 0)),
    ]
    for place, step in enumerate((1, -1, 3, -5, 5, -3)):
        slots.append((slot_of(step, core), at(8, place)))
    for place, (slot, part) in enumerate(slots):
        couple(place, slot, part)
    for place, (slot, part) in enumerate(slots):
        pltpu.make_async_copy(stage.at[place], out.at[slot], sem.at[place]).wait()


VMEM = pl.BlockSpec(memory_space=pltpu.VMEM)
SMEM = pl.BlockSpec(memory_space=pltpu.SMEM)
ANY = pl.BlockSpec(memory_space=pl.ANY)


def f32(*shape):
    return jax.ShapeDtypeStruct(shape, F32)


def b16(*shape):
    return jax.ShapeDtypeStruct(shape, BF16)


def call(kernel, outs, *args, scratch=(), out_specs=None):
    tables = 0
    body = kernel
    if isinstance(args[0], list):
        tables = len(args[0])
        args = (*args[0], *args[1:])

        def body(*refs):
            kernel(refs[:tables], *refs[tables:])

    return pl.pallas_call(
        body,
        out_shape=tuple(outs),
        in_specs=[SMEM] * tables + [VMEM] * (len(args) - tables),
        out_specs=tuple(out_specs or [VMEM] * len(outs)),
        scratch_shapes=list(scratch),
        compiler_params=pltpu.CompilerParams(vmem_limit_bytes=16 * 2**20),
        cost_estimate=pl.CostEstimate(flops=1, bytes_accessed=1, transcendentals=0),
    )(*args)


def on_device(local_operator, coarse_basis, neighbour_links, margin_blocks):
    matrix = local_operator[0, 0]
    initial = coarse_basis[0, 0]
    n, columns = initial.shape
    width = BLK
    assert columns == 2 * width
    place = lax.axis_index("sub")
    core = place % 2
    y = (place // 2) % RING
    wrapped = (y == jnp.where(core == 0, 0, RING - 1)).astype(jnp.int32)
    own = jnp.concatenate(
        [
            margin_blocks.reshape(2 * SLOTS),
            neighbour_links.reshape(2 * REACH),
            jnp.ones((2,), jnp.int32),
            jnp.stack([core, wrapped]),
        ]
    )
    tab = [own, send(own, route_core), send(own, route_ring)]

    full, pair, one = f32(n, width), f32(4 * BLK, width), f32(2 * BLK, width)
    square = f32(width, width)
    packed = [pair, one, one, one]

    def depart(block, near, far, up, down):
        return [
            send(block, route_ring),
            send(near, route_near),
            send(far, route_far),
            send_group(down, -1),
            send_group(up, 1),
        ]

    def arrive(block, first, cross, outs):
        ring, near, far, above, below = first
        ahead, back, layer = call(relay_kernel, [pair, pair, pair], tab, ring)
        ahead = send(ahead, route_ahead)
        back = send(back, route_back)
        layer = send(layer, route_layer)
        parts = [ring, near, far, ahead, back, layer, above, below]
        theirs, *rest = call(cross, outs, tab, block, *parts)
        return parts, rest, send(theirs, route_core)

    def summed(block, first):
        _, (mine,), theirs = arrive(block, first, cross_sum_kernel, [full, full])
        return mine, theirs

    def copied(block, first):
        parts, _, theirs = arrive(block, first, cross_copy_kernel, [f32(12 * BLK, width)])
        return parts + [theirs]

    high, low, scale, block0 = call(
        start_kernel, [b16(n, n), b16(n, n), full, full], matrix, initial
    )
    block0, *tab = lax.optimization_barrier((block0, *tab))
    block1, *packets = call(
        next_kernel, [full, *packed, *packed], tab, high, low, initial, block0
    )
    sent0, sent1 = [block0, *packets[:4]], [block1, *packets[4:]]
    first0 = depart(*sent0)
    first1 = depart(*sent1)

    def sweep(column, block, first):
        return call(
            functools.partial(sweep_kernel, column),
            [full, full, *packed],
            tab,
            high,
            low,
            scale,
            initial,
            *summed(block, first),
        )

    x0, *sent0 = sweep(0, sent0[0], first0)
    first0 = depart(*sent0)
    x1, *sent1 = sweep(1, sent1[0], first1)
    first1 = depart(*sent1)

    x0, product0, inverse0, scaled0, *packets0 = call(
        first_factor_kernel,
        [full, full, square, full, *packed],
        tab,
        high,
        low,
        scale,
        x0,
        *summed(sent0[0], first0),
    )
    first0 = depart(scaled0, *packets0)
    smoothed, product1, lower, rest = call(
        second_product_kernel,
        [f32(n, columns), full, square, square],
        high,
        low,
        scale,
        x1,
        *summed(sent1[0], first1),
        x0,
        product0,
        inverse0,
    )
    inverse1, scaled1, *packets1 = call(
        second_factor_kernel,
        [square, full, *packed],
        tab,
        product1,
        lower,
        rest,
        scaled0,
    )
    first1 = depart(scaled1, *packets1)
    turned = b16(n // BLK, columns, BLK)
    basis = call(
        basis_kernel, [turned, turned], smoothed, lower, inverse0, inverse1
    )
    received0 = copied(scaled0, first0)
    received1 = copied(scaled1, first1)
    (coupling,) = call(
        coupling_kernel,
        [f32(SLOTS, columns, columns)],
        tab,
        *basis,
        *received0,
        *received1,
        scratch=[
            pltpu.VMEM((SLOTS, columns, columns), F32),
            pltpu.SemaphoreType.DMA((SLOTS,)),
        ],
        out_specs=[ANY],
    )
    return (smoothed[None, None], coupling[None, None])


def solution(mesh):
    in_specs = (
        P("sub", "grp", None, None),
        P("sub", "grp", None, None),
        P("sub", "grp", None),
        P("sub", "grp", None, None),
    )
    out_specs = (P("sub", "grp", None, None), P("sub", "grp", None, None, None))
    return jax.shard_map(
        on_device, mesh=mesh, in_specs=in_specs, out_specs=out_specs, check_vma=False
    )
```

```python
import functools
import math

import jax
import jax.numpy as jnp
from jax import lax
from jax.experimental import pallas as pl
from jax.experimental.pallas import tpu as pltpu
from jax.sharding import PartitionSpec as P

BLK = 128
REACH = 6
SLOTS = 2 * REACH + 2
RING = 4
OWN, OTHER, SOURCE = range(3)
CORE = 3 * SLOTS
WRAPS = CORE + 1
F32 = jnp.float32
BF16 = jnp.bfloat16


def sign(i):
    return 1 - 2 * (i % 2)


def along_ring(i, step):
    core, y, z = i % 2, (i // 2) % RING, i // (2 * RING)
    return (z * RING + (y + step) % RING) * 2 + core


def wraps(i):
    y = (i // 2) % RING
    return y == (0 if i % 2 == 0 else RING - 1)


def route_ring(i):
    return along_ring(i, sign(i))


def route_source(i):
    return along_ring(i, -sign(i))


def route_near(i):
    return i - 2 * sign(i)


def route_far(i):
    return i + 6 * sign(i)


def route_ahead(i):
    return route_source(i) + 4 * sign(i)


def route_back(i):
    return route_source(i) - 4 * sign(i)


def route_layer(i):
    return route_source(i) + (2 if wraps(i) else -6) * sign(i)


def route_core(i):
    return i ^ 1


def send(block, route):
    n = lax.axis_size("sub")
    return lax.ppermute(block, "sub", [(i, route(i) % n) for i in range(n)])


def send_group(block, distance):
    n = lax.axis_size("grp")
    return lax.ppermute(block, "grp", [(i, (i + distance) % n) for i in range(n)])


def slot_of(step, core):
    up = step - 1 if step > 0 else REACH - 1 - step
    down = REACH - 1 + step if step > 0 else -step - 1
    return jnp.where(core == 0, up, down)


def rows_of(tab, base, slot, j):
    return pl.ds(pl.multiple_of(tab[base][2 * slot + j] * BLK, BLK), BLK)


def flag_of(tab, base, slot):
    return tab[base][2 * SLOTS + slot].astype(F32)


def pick(tab, base, slot, source, target, place):
    for j in range(2):
        target[pl.ds((2 * place + j) * BLK, BLK), :] = source[rows_of(tab, base, slot, j), :]


def halves(x):
    high = x.astype(BF16)
    return high, (x - high.astype(F32)).astype(BF16)


def dot(a, b, dims=((1,), (0,))):
    return lax.dot_general(a, b, (dims, ((), ())), preferred_element_type=F32)


def dot_full(a, b, dims=((1,), (0,))):
    return lax.dot_general(
        a, b, (dims, ((), ())), precision=lax.Precision.HIGHEST, preferred_element_type=F32
    )


def dot_split(a, b, dims=((1,), (0,))):
    a_high, a_low = halves(a)
    b_high, b_low = halves(b)
    return dot(a_high, b_high, dims) + dot(a_high, b_low, dims) + dot(a_low, b_high, dims)


def apply_operator(high, low, x, out):
    x_high, x_low = halves(x)
    width = x.shape[1]
    both = jnp.concatenate([x_high, x_low], axis=1)
    step = 256
    for r in range(0, high.shape[0], step):
        first = dot(high[r : r + step, :], both)
        out[r : r + step, :] = (
            first[:, :width] + first[:, width:] + dot(low[r : r + step, :], x_high)
        )


def pack_near(tab, full, near):
    core = tab[OWN][CORE]
    pick(tab, OWN, slot_of(-2, core), full, near, 0)
    pick(tab, OWN, slot_of(-1, core), full, near, 1)


def pack_wide(tab, halves_of, far, up, down):
    core = tab[OWN][CORE]
    for h, full in enumerate(halves_of):
        pick(tab, OWN, slot_of(6, core), full, far, h)
        pick(tab, OWN, 2 * REACH, full, up, h)
        pick(tab, OWN, 2 * REACH + 1, full, down, h)


def start_kernel(a, x, high, low, scale, full):
    n = a.shape[0]
    step = 2 * BLK
    x_high, x_low = halves(x[:, :BLK])
    both = jnp.concatenate([x_high, x_low], axis=1)
    eye = (
        lax.broadcasted_iota(jnp.int32, (BLK, BLK), 0)
        == lax.broadcasted_iota(jnp.int32, (BLK, BLK), 1)
    )
    for r in range(0, n, step):
        row_high, row_low = halves(a[r : r + step, :])
        high[r : r + step, :] = row_high
        low[r : r + step, :] = row_low
        first = dot(row_high, both)
        full[r : r + step, :] = first[:, :BLK] + first[:, BLK:] + dot(row_low, x_high)
        for d in range(r, r + step, BLK):
            square = a[d : d + BLK, d : d + BLK]
            diagonal = jnp.sum(jnp.where(eye, square, 0.0), axis=1, keepdims=True)
            scale[d : d + BLK, :] = jnp.broadcast_to(0.5 / diagonal, (BLK, BLK))


def next_kernel(tab, high, low, x, first, full, near0, near1, *wide):
    pack_near(tab, first, near0)
    apply_operator(high, low, x[:, BLK:], full)
    pack_near(tab, full, near1)
    pack_wide(tab, (first, full), *wide)


def relay_kernel(tab, ring, ahead, back, layer):
    core, wrapped = tab[OWN][CORE], tab[OWN][WRAPS]
    pick(tab, SOURCE, slot_of(4, core), ring, ahead, 0)
    pick(tab, SOURCE, slot_of(5, core), ring, ahead, 1)
    pick(tab, SOURCE, slot_of(-4, core), ring, back, 0)
    pick(tab, SOURCE, slot_of(-3, core), ring, back, 1)
    mine = jnp.where(wrapped == 1, slot_of(2, core), slot_of(-6, core))
    theirs = jnp.where(wrapped == 1, slot_of(3, core), slot_of(-5, core))
    pick(tab, SOURCE, mine, ring, layer, 0)
    pick(tab, SOURCE, theirs, ring, layer, 1)


def add_rows(tab, base, slot, total, part):
    flag = flag_of(tab, base, slot)
    for j in range(2):
        rows = rows_of(tab, base, slot, j)
        total[rows, :] += flag * part(j)


def packet(ref, place):
    return lambda j: ref[pl.ds((2 * place + j) * BLK, BLK), :]


def block_rows(tab, base, slot, ref):
    return lambda j: ref[rows_of(tab, base, slot, j), :]


def cross_sum_kernel(h, tab, full, ring, near, far, ahead, back, layer, above, below, total, mine):
    core, wrapped = tab[OWN][CORE], tab[OWN][WRAPS]
    other = 1 - core
    total[...] = jnp.zeros(total.shape, F32)
    add = functools.partial(add_rows, tab, OTHER)
    add(slot_of(1, other), total, block_rows(tab, OWN, slot_of(1, core), full))
    add(slot_of(-1, other), total, packet(near, 1))
    here = jnp.where(wrapped == 1, slot_of(-5, core), slot_of(3, core))
    at = jnp.where(wrapped == 1, slot_of(-5, other), slot_of(3, other))
    add(at, total, block_rows(tab, SOURCE, here, ring))
    at = jnp.where(wrapped == 1, slot_of(3, other), slot_of(-5, other))
    add(at, total, packet(layer, 1))
    add(slot_of(5, other), total, packet(ahead, 1))
    add(slot_of(-3, other), total, packet(back, 1))
    mine[...] = full[...]
    add = functools.partial(add_rows, tab, OWN)
    add(slot_of(2, core), mine, packet(near, 0))
    add(slot_of(-6, core), mine, packet(far, h))
    here = jnp.where(wrapped == 1, slot_of(-6, core), slot_of(2, core))
    at = jnp.where(wrapped == 1, slot_of(6, core), slot_of(-2, core))
    add(at, mine, block_rows(tab, SOURCE, here, ring))
    at = jnp.where(wrapped == 1, slot_of(-2, core), slot_of(6, core))
    add(at, mine, packet(layer, 0))
    add(slot_of(-4, core), mine, packet(ahead, 0))
    add(slot_of(4, core), mine, packet(back, 0))
    add(2 * REACH, mine, packet(above, h))
    add(2 * REACH + 1, mine, packet(below, h))


def cross_copy_kernel(h, tab, full, ring, near, far, ahead, back, layer, above, below, out):
    core, wrapped = tab[OWN][CORE], tab[OWN][WRAPS]
    half = 2 * BLK
    pick(tab, OWN, slot_of(1, core), full, out, 0)
    out[half : 2 * half, :] = near[half:, :]
    here = jnp.where(wrapped == 1, slot_of(-5, core), slot_of(3, core))
    for j in range(2):
        local = ring[rows_of(tab, SOURCE, here, j), :]
        far = layer[half + j * BLK : half + (j + 1) * BLK, :]
        at = 2 * half + j * BLK
        out[at : at + BLK, :] = jnp.where(wrapped == 1, far, local)
        out[at + half : at + half + BLK, :] = jnp.where(wrapped == 1, local, far)
    out[4 * half : 5 * half, :] = ahead[half:, :]
    out[5 * half : 6 * half, :] = back[half:, :]


def inverse_factor(gram):
    tile = 8
    count = BLK // tile
    row_id = lax.broadcasted_iota(jnp.int32, (tile, BLK), 0)
    lane_id = lax.broadcasted_iota(jnp.int32, (tile, BLK), 1)
    eye = (
        lax.broadcasted_iota(jnp.int32, (BLK, BLK), 0)
        == lax.broadcasted_iota(jnp.int32, (BLK, BLK), 1)
    )
    diagonal = jnp.where(eye, gram, 0.0)
    left = lax.rsqrt(jnp.sum(diagonal, axis=1, keepdims=True))
    top = lax.rsqrt(jnp.sum(diagonal, axis=0, keepdims=True))
    unit = gram * left * top
    g = [unit[tile * i : tile * i + tile, :] for i in range(count)]
    w = [jnp.where(lane_id == row_id + tile * i, 1.0, 0.0).astype(F32) for i in range(count)]

    def columns(t, base):
        return [jnp.broadcast_to(t[:, base + q : base + q + 1], (tile, BLK)) for q in range(tile)]

    def row(t, r):
        return jnp.broadcast_to(t[r : r + 1, :], (tile, BLK))

    def total(terms):
        while len(terms) > 1:
            terms = [terms[j] + terms[j + 1] for j in range(0, len(terms), 2)]
        return terms[0]

    for b in range(count):
        cols = columns(g[b], tile * b)
        pg, pw = g[b], w[b]
        inv = jnp.ones((tile, BLK), F32)
        for q in range(0, tile, 2):
            c0, c1 = cols[q], cols[q + 1]
            a00, a01, a11 = row(c0, q), row(c1, q), row(c1, q + 1)
            inv0 = 1.0 / a00
            inv_det = 1.0 / (a00 * a11 - a01 * a01)
            inv = jnp.where(row_id == q, inv0, jnp.where(row_id == q + 1, a00 * inv_det, inv))
            below = row_id > q + 1
            step0 = jnp.where(
                below, (c0 * a11 - c1 * a01) * inv_det, jnp.where(row_id == q + 1, a01 * inv0, 0.0)
            )
            step1 = jnp.where(below, (c1 * a00 - c0 * a01) * inv_det, 0.0)

            def reduce(t):
                return t - step0 * row(t, q) - step1 * row(t, q + 1)

            for m in range(q + 1, tile):
                cols[m] = reduce(cols[m])
            pg, pw = reduce(pg), reduce(pw)
        w[b] = pw * jnp.sqrt(inv)
        if b == count - 1:
            break
        zg, zw = pg * inv, pw * inv
        for q in range(tile - 1, 0, -1):
            back = jnp.where(row_id < q, cols[q] * inv, 0.0)
            zg, zw = zg - back * row(zg, q), zw - back * row(zw, q)
        rows_g = [row(zg, q) for q in range(tile)]
        rows_w = [row(zw, q) for q in range(tile)]
        for i in range(b + 1, count):
            cs = columns(g[i], tile * b)
            g[i] = g[i] - total([c * z for c, z in zip(cs, rows_g)])
            w[i] = w[i] - total([c * z for c, z in zip(cs, rows_w)])
    return jnp.concatenate(w, axis=0) * top


def first_sweep_kernel(tab, high, low, scale, x, mine, cross, x_new, full, near):
    x_new[...] = x[:, :BLK] - (mine[...] + cross[...]) * scale[...]
    apply_operator(high, low, x_new[...], full)
    pack_near(tab, full, near)


def second_sweep_kernel(
    tab, high, low, scale, x, mine, cross, first, x_new, full, near, *wide
):
    x_new[...] = x[:, BLK:] - (mine[...] + cross[...]) * scale[...]
    apply_operator(high, low, x_new[...], full)
    pack_near(tab, full, near)
    pack_wide(tab, (first, full), *wide)


def symmetric(g):
    return 0.5 * (g + g.T)


ROWS = ((0,), (0,))
LANES = ((1,), (1,))


def first_factor_kernel(tab, high, low, scale, x, mine, cross, *outs):
    x_new, product, inverse, scaled, near = outs
    x_new[...] = x[...] - (mine[...] + cross[...]) * scale[...]
    apply_operator(high, low, x_new[...], product)
    gram = symmetric(dot_full(x_new[...], product[...], ROWS))
    inverse[...] = inverse_factor(gram)
    scaled[...] = dot_split(product[...], inverse[...], LANES)
    pack_near(tab, scaled, near)


def second_product_kernel(
    high, low, scale, x, mine, cross, x0, product0, inverse0, x_out, product, lower, rest
):
    x_new = x[...] - (mine[...] + cross[...]) * scale[...]
    x_out[:, :BLK] = x0[...]
    x_out[:, BLK:] = x_new
    apply_operator(high, low, x_new, product)
    corner = 0.5 * (
        dot_full(x_new, product0[...], ROWS) + dot_full(product[...], x0[...], ROWS)
    )
    side = dot_full(corner, inverse0[...], LANES)
    lower[...] = side
    gram = symmetric(dot_full(x_new, product[...], ROWS))
    rest[...] = gram - dot_full(side, side, LANES)


def second_factor_kernel(
    tab, product, lower, rest, scaled0, inverse, scaled, near, *wide
):
    inverse[...] = inverse_factor(rest[...])
    change = product[...] - dot_split(scaled0[...], lower[...], LANES)
    scaled[...] = dot_split(change, inverse[...], LANES)
    pack_near(tab, scaled, near)
    pack_wide(tab, (scaled0, scaled), *wide)


def basis_kernel(x, lower, inverse0, inverse, basis_high, basis_low):
    basis0 = dot_split(x[:, :BLK], inverse0[...], LANES)
    change = x[:, BLK:] - dot_split(basis0, lower[...], LANES)
    basis1 = dot_split(change, inverse[...], LANES)
    factor = math.sqrt(x.shape[0])
    for b in range(x.shape[0] // BLK):
        rows = slice(b * BLK, (b + 1) * BLK)
        for h, part in enumerate((basis0[rows], basis1[rows])):
            block_high, block_low = halves(factor * part.T)
            basis_high[b, h * BLK : (h + 1) * BLK, :] = block_high
            basis_low[b, h * BLK : (h + 1) * BLK, :] = block_low


def coupling_kernel(tab, basis_high, basis_low, *refs):
    received = (refs[:9], refs[9:18])
    out, stage, sem = refs[18:]
    core, wrapped = tab[OWN][CORE], tab[OWN][WRAPS]
    local = jnp.where(wrapped == 1, slot_of(-6, core), slot_of(2, core))

    def couple(place, slot, part):
        flag = flag_of(tab, OWN, slot)
        first, second = tab[OWN][2 * slot], tab[OWN][2 * slot + 1]
        left_high = jnp.concatenate([basis_high[first], basis_high[second]], axis=1)
        left_low = jnp.concatenate([basis_low[first], basis_low[second]], axis=1)
        for h in range(2):
            right = jnp.concatenate([part(h, 0), part(h, 1)], axis=0)
            right_high, right_low = halves(right)
            both = jnp.concatenate([right_high, right_low], axis=1)
            whole = dot(left_high, both)
            value = whole[:, :BLK] + whole[:, BLK:] + dot(left_low, right_high)
            stage[place, :, h * BLK : (h + 1) * BLK] = flag * value
        pltpu.make_async_copy(stage.at[place], out.at[slot], sem.at[place]).start()

    def at(index, place):
        start = 2 * place * BLK
        return lambda h, j: received[h][index][start + j * BLK : start + (j + 1) * BLK, :]

    def wide(index):
        return lambda h, j: received[h][index][(2 * h + j) * BLK : (2 * h + j + 1) * BLK, :]

    def from_ring(h, j):
        return received[h][0][rows_of(tab, SOURCE, local, j), :]

    slots = [
        (2 * REACH, wide(6)),
        (2 * REACH + 1, wide(7)),
        (slot_of(2, core), at(1, 0)),
        (slot_of(-6, core), wide(2)),
        (jnp.where(wrapped == 1, slot_of(6, core), slot_of(-2, core)), from_ring),
        (jnp.where(wrapped == 1, slot_of(-2, core), slot_of(6, core)), at(5, 0)),
        (slot_of(-4, core), at(3, 0)),
        (slot_of(4, core), at(4, 0)),
    ]
    for place, step in enumerate((1, -1, 3, -5, 5, -3)):
        slots.append((slot_of(step, core), at(8, place)))
    for place, (slot, part) in enumerate(slots):
        couple(place, slot, part)
    for place, (slot, part) in enumerate(slots):
        pltpu.make_async_copy(stage.at[place], out.at[slot], sem.at[place]).wait()


VMEM = pl.BlockSpec(memory_space=pltpu.VMEM)
SMEM = pl.BlockSpec(memory_space=pltpu.SMEM)
ANY = pl.BlockSpec(memory_space=pl.ANY)


def f32(*shape):
    return jax.ShapeDtypeStruct(shape, F32)


def b16(*shape):
    return jax.ShapeDtypeStruct(shape, BF16)


def call(kernel, outs, *args, scratch=(), out_specs=None):
    tables = 0
    body = kernel
    if isinstance(args[0], list):
        tables = len(args[0])
        args = (*args[0], *args[1:])

        def body(*refs):
            kernel(refs[:tables], *refs[tables:])

    return pl.pallas_call(
        body,
        out_shape=tuple(outs),
        in_specs=[SMEM] * tables + [VMEM] * (len(args) - tables),
        out_specs=tuple(out_specs or [VMEM] * len(outs)),
        scratch_shapes=list(scratch),
        compiler_params=pltpu.CompilerParams(vmem_limit_bytes=16 * 2**20),
        cost_estimate=pl.CostEstimate(flops=1, bytes_accessed=1, transcendentals=0),
    )(*args)


def on_device(local_operator, coarse_basis, neighbour_links, margin_blocks):
    matrix = local_operator[0, 0]
    initial = coarse_basis[0, 0]
    n, columns = initial.shape
    width = BLK
    assert columns == 2 * width
    place = lax.axis_index("sub")
    core = place % 2
    y = (place // 2) % RING
    wrapped = (y == jnp.where(core == 0, 0, RING - 1)).astype(jnp.int32)
    own = jnp.concatenate(
        [
            margin_blocks.reshape(2 * SLOTS),
            neighbour_links.reshape(2 * REACH),
            jnp.ones((2,), jnp.int32),
            jnp.stack([core, wrapped]),
        ]
    )
    tab = [own, send(own, route_core), send(own, route_ring)]

    full, pair = f32(n, width), f32(4 * BLK, width)
    square = f32(width, width)
    wide = [pair, pair, pair]

    def depart(up, down):
        return send_group(down, -1), send_group(up, 1)

    def forward(cut):
        ahead, back, layer = cut
        return send(ahead, route_ahead), send(back, route_back), send(layer, route_layer)

    def relay(ring0, ring1, near0, near1, far, hold):
        cut0 = call(relay_kernel, [pair, pair, pair], tab, ring0)
        if hold:
            ring1, near0, *cut0 = lax.optimization_barrier((ring1, near0, *cut0))
        cut1 = call(relay_kernel, [pair, pair, pair], tab, ring1)
        if hold:
            near1, far, *cut1 = lax.optimization_barrier((near1, far, *cut1))
        ring0, *cut1 = lax.optimization_barrier((ring0, *cut1))
        direct = send(near0, route_near), send(near1, route_near), send(far, route_far)
        return ring0, (forward(cut0), forward(cut1)), *direct

    def arrive(kernel, h, outs, block, ring, near, relayed, spread):
        ahead, back, layer = relayed
        far, above, below = spread
        parts = [ring, near, far, ahead, back, layer, above, below]
        theirs, *rest = call(functools.partial(kernel, h), outs, tab, block, *parts)
        return parts, rest, send(theirs, route_core)

    def summed(h, *moved):
        _, (mine,), theirs = arrive(cross_sum_kernel, h, [full, full], *moved)
        return mine, theirs

    def copied(h, *moved):
        parts, _, theirs = arrive(cross_copy_kernel, h, [f32(12 * BLK, width)], *moved)
        return parts + [theirs]

    high, low, scale, block0 = call(
        start_kernel, [b16(n, n), b16(n, n), full, full], matrix, initial
    )
    block0, *tab = lax.optimization_barrier((block0, *tab))
    ring0 = send(block0, route_ring)
    block1, near0, near1, *packets = call(
        next_kernel, [full, pair, pair, *wide], tab, high, low, initial, block0
    )
    ring1 = send(block1, route_ring)
    far, *packets = packets
    spread = depart(*packets)
    ring0, relayed, near0, near1, far = relay(
        ring0, ring1, near0, near1, far, True
    )
    spread = (far, *spread)
    sums0 = summed(0, block0, ring0, near0, relayed[0], spread)
    sums1 = summed(1, block1, ring1, near1, relayed[1], spread)

    x0, block0, near0 = call(
        first_sweep_kernel, [full, full, pair], tab, high, low, scale, initial, *sums0
    )
    ring0 = send(block0, route_ring)
    x1, block1, near1, *packets = call(
        second_sweep_kernel,
        [full, full, pair, *wide],
        tab,
        high,
        low,
        scale,
        initial,
        *sums1,
        block0,
    )
    ring1 = send(block1, route_ring)
    far, *packets = packets
    spread = depart(*packets)
    ring0, relayed, near0, near1, far = relay(
        ring0, ring1, near0, near1, far, True
    )
    spread = (far, *spread)
    sums0 = summed(0, block0, ring0, near0, relayed[0], spread)

    x0, product0, inverse0, scaled0, near0 = call(
        first_factor_kernel,
        [full, full, square, full, pair],
        tab,
        high,
        low,
        scale,
        x0,
        *sums0,
    )
    ring0 = send(scaled0, route_ring)
    ring1, scaled0 = lax.optimization_barrier((ring1, scaled0))
    sums1 = summed(1, block1, ring1, near1, relayed[1], spread)
    smoothed, product1, lower, rest = call(
        second_product_kernel,
        [f32(n, columns), full, square, square],
        high,
        low,
        scale,
        x1,
        *sums1,
        x0,
        product0,
        inverse0,
    )
    inverse1, scaled1, near1, *packets = call(
        second_factor_kernel,
        [square, full, pair, *wide],
        tab,
        product1,
        lower,
        rest,
        scaled0,
    )
    leaving1, ring0 = lax.optimization_barrier((scaled1, ring0))
    ring1 = send(leaving1, route_ring)
    far, *packets = packets
    spread = depart(*packets)
    turned = b16(n // BLK, columns, BLK)
    basis = call(basis_kernel, [turned, turned], smoothed, lower, inverse0, inverse1)
    ring0, relayed, near0, near1, far = relay(
        ring0, ring1, near0, near1, far, False
    )
    spread = (far, *spread)
    received0 = copied(0, scaled0, ring0, near0, relayed[0], spread)
    received1 = copied(1, scaled1, ring1, near1, relayed[1], spread)
    (coupling,) = call(
        coupling_kernel,
        [f32(SLOTS, columns, columns)],
        tab,
        *basis,
        *received0,
        *received1,
        scratch=[
            pltpu.VMEM((SLOTS, columns, columns), F32),
            pltpu.SemaphoreType.DMA((SLOTS,)),
        ],
        out_specs=[ANY],
    )
    return (smoothed[None, None], coupling[None, None])


def solution(mesh):
    in_specs = (
        P("sub", "grp", None, None),
        P("sub", "grp", None, None),
        P("sub", "grp", None),
        P("sub", "grp", None, None),
    )
    out_specs = (P("sub", "grp", None, None), P("sub", "grp", None, None, None))
    return jax.shard_map(
        on_device, mesh=mesh, in_specs=in_specs, out_specs=out_specs, check_vma=False
    )
```

```python
import functools
import math

import jax
import jax.numpy as jnp
from jax import lax
from jax.experimental import pallas as pl
from jax.experimental.pallas import tpu as pltpu
from jax.sharding import PartitionSpec as P

BLK = 128
REACH = 6
SLOTS = 2 * REACH + 2
RING = 4
OWN, OTHER, SOURCE = range(3)
CORE = 3 * SLOTS
WRAPS = CORE + 1
F32 = jnp.float32
BF16 = jnp.bfloat16


def sign(i):
    return 1 - 2 * (i % 2)


def along_ring(i, step):
    core, y, z = i % 2, (i // 2) % RING, i // (2 * RING)
    return (z * RING + (y + step) % RING) * 2 + core


def wraps(i):
    y = (i // 2) % RING
    return y == (0 if i % 2 == 0 else RING - 1)


def route_ring(i):
    return along_ring(i, sign(i))


def route_source(i):
    return along_ring(i, -sign(i))


def route_near(i):
    return i - 2 * sign(i)


def route_far(i):
    return i + 6 * sign(i)


def route_ahead(i):
    return route_source(i) + 4 * sign(i)


def route_back(i):
    return route_source(i) - 4 * sign(i)


def route_layer(i):
    return route_source(i) + (2 if wraps(i) else -6) * sign(i)


def route_core(i):
    return i ^ 1


def send(block, route):
    n = lax.axis_size("sub")
    return lax.ppermute(block, "sub", [(i, route(i) % n) for i in range(n)])


def send_group(block, distance):
    n = lax.axis_size("grp")
    return lax.ppermute(block, "grp", [(i, (i + distance) % n) for i in range(n)])


def slot_of(step, core):
    up = step - 1 if step > 0 else REACH - 1 - step
    down = REACH - 1 + step if step > 0 else -step - 1
    return jnp.where(core == 0, up, down)


def rows_of(tab, base, slot, j):
    return pl.ds(pl.multiple_of(tab[base][2 * slot + j] * BLK, BLK), BLK)


def flag_of(tab, base, slot):
    return tab[base][2 * SLOTS + slot].astype(F32)


def pick(tab, base, slot, source, target, place):
    for j in range(2):
        target[pl.ds((2 * place + j) * BLK, BLK), :] = source[rows_of(tab, base, slot, j), :]


def halves(x):
    high = x.astype(BF16)
    return high, (x - high.astype(F32)).astype(BF16)


def dot(a, b, dims=((1,), (0,))):
    return lax.dot_general(a, b, (dims, ((), ())), preferred_element_type=F32)


def dot_full(a, b, dims=((1,), (0,))):
    return lax.dot_general(
        a, b, (dims, ((), ())), precision=lax.Precision.HIGHEST, preferred_element_type=F32
    )


def dot_split(a, b, dims=((1,), (0,))):
    a_high, a_low = halves(a)
    b_high, b_low = halves(b)
    return dot(a_high, b_high, dims) + dot(a_high, b_low, dims) + dot(a_low, b_high, dims)


def apply_operator(high, low, x, out):
    x_high, x_low = halves(x)
    width = x.shape[1]
    both = jnp.concatenate([x_high, x_low], axis=1)
    step = 256
    for r in range(0, high.shape[0], step):
        first = dot(high[r : r + step, :], both)
        out[r : r + step, :] = (
            first[:, :width] + first[:, width:] + dot(low[r : r + step, :], x_high)
        )


def pack_near(tab, full, near):
    core = tab[OWN][CORE]
    pick(tab, OWN, slot_of(-2, core), full, near, 0)
    pick(tab, OWN, slot_of(-1, core), full, near, 1)


def pack_wide(tab, halves_of, far, up, down):
    core = tab[OWN][CORE]
    for h, full in enumerate(halves_of):
        pick(tab, OWN, slot_of(6, core), full, far, h)
        pick(tab, OWN, 2 * REACH, full, up, h)
        pick(tab, OWN, 2 * REACH + 1, full, down, h)


def start_kernel(a, x, high, low, scale, full):
    n = a.shape[0]
    step = 2 * BLK
    x_high, x_low = halves(x[:, :BLK])
    both = jnp.concatenate([x_high, x_low], axis=1)
    eye = (
        lax.broadcasted_iota(jnp.int32, (BLK, BLK), 0)
        == lax.broadcasted_iota(jnp.int32, (BLK, BLK), 1)
    )
    for r in range(0, n, step):
        row_high, row_low = halves(a[r : r + step, :])
        high[r : r + step, :] = row_high
        low[r : r + step, :] = row_low
        first = dot(row_high, both)
        full[r : r + step, :] = first[:, :BLK] + first[:, BLK:] + dot(row_low, x_high)
        for d in range(r, r + step, BLK):
            square = a[d : d + BLK, d : d + BLK]
            diagonal = jnp.sum(jnp.where(eye, square, 0.0), axis=1, keepdims=True)
            scale[d : d + BLK, :] = jnp.broadcast_to(0.5 / diagonal, (BLK, BLK))


def next_kernel(tab, high, low, x, first, full, near0, near1, *wide):
    pack_near(tab, first, near0)
    apply_operator(high, low, x[:, BLK:], full)
    pack_near(tab, full, near1)
    pack_wide(tab, (first, full), *wide)


def relay_kernel(tab, ring, ahead, back, layer):
    core, wrapped = tab[OWN][CORE], tab[OWN][WRAPS]
    pick(tab, SOURCE, slot_of(4, core), ring, ahead, 0)
    pick(tab, SOURCE, slot_of(5, core), ring, ahead, 1)
    pick(tab, SOURCE, slot_of(-4, core), ring, back, 0)
    pick(tab, SOURCE, slot_of(-3, core), ring, back, 1)
    mine = jnp.where(wrapped == 1, slot_of(2, core), slot_of(-6, core))
    theirs = jnp.where(wrapped == 1, slot_of(3, core), slot_of(-5, core))
    pick(tab, SOURCE, mine, ring, layer, 0)
    pick(tab, SOURCE, theirs, ring, layer, 1)


def add_rows(tab, base, slot, total, part):
    flag = flag_of(tab, base, slot)
    for j in range(2):
        rows = rows_of(tab, base, slot, j)
        total[rows, :] += flag * part(j)


def packet(ref, place):
    return lambda j: ref[pl.ds((2 * place + j) * BLK, BLK), :]


def block_rows(tab, base, slot, ref):
    return lambda j: ref[rows_of(tab, base, slot, j), :]


def cross_sum_kernel(h, tab, full, ring, near, far, ahead, back, layer, above, below, total, mine):
    core, wrapped = tab[OWN][CORE], tab[OWN][WRAPS]
    other = 1 - core
    total[...] = jnp.zeros(total.shape, F32)
    add = functools.partial(add_rows, tab, OTHER)
    add(slot_of(1, other), total, block_rows(tab, OWN, slot_of(1, core), full))
    add(slot_of(-1, other), total, packet(near, 1))
    here = jnp.where(wrapped == 1, slot_of(-5, core), slot_of(3, core))
    at = jnp.where(wrapped == 1, slot_of(-5, other), slot_of(3, other))
    add(at, total, block_rows(tab, SOURCE, here, ring))
    at = jnp.where(wrapped == 1, slot_of(3, other), slot_of(-5, other))
    add(at, total, packet(layer, 1))
    add(slot_of(5, other), total, packet(ahead, 1))
    add(slot_of(-3, other), total, packet(back, 1))
    mine[...] = full[...]
    add = functools.partial(add_rows, tab, OWN)
    add(slot_of(2, core), mine, packet(near, 0))
    add(slot_of(-6, core), mine, packet(far, h))
    here = jnp.where(wrapped == 1, slot_of(-6, core), slot_of(2, core))
    at = jnp.where(wrapped == 1, slot_of(6, core), slot_of(-2, core))
    add(at, mine, block_rows(tab, SOURCE, here, ring))
    at = jnp.where(wrapped == 1, slot_of(-2, core), slot_of(6, core))
    add(at, mine, packet(layer, 0))
    add(slot_of(-4, core), mine, packet(ahead, 0))
    add(slot_of(4, core), mine, packet(back, 0))
    add(2 * REACH, mine, packet(above, h))
    add(2 * REACH + 1, mine, packet(below, h))


def cross_copy_kernel(h, tab, full, ring, near, far, ahead, back, layer, above, below, out):
    core, wrapped = tab[OWN][CORE], tab[OWN][WRAPS]
    half = 2 * BLK
    pick(tab, OWN, slot_of(1, core), full, out, 0)
    out[half : 2 * half, :] = near[half:, :]
    here = jnp.where(wrapped == 1, slot_of(-5, core), slot_of(3, core))
    for j in range(2):
        local = ring[rows_of(tab, SOURCE, here, j), :]
        far = layer[half + j * BLK : half + (j + 1) * BLK, :]
        at = 2 * half + j * BLK
        out[at : at + BLK, :] = jnp.where(wrapped == 1, far, local)
        out[at + half : at + half + BLK, :] = jnp.where(wrapped == 1, local, far)
    out[4 * half : 5 * half, :] = ahead[half:, :]
    out[5 * half : 6 * half, :] = back[half:, :]


def inverse_factor(gram):
    tile = 8
    count = BLK // tile
    row_id = lax.broadcasted_iota(jnp.int32, (tile, BLK), 0)
    lane_id = lax.broadcasted_iota(jnp.int32, (tile, BLK), 1)
    eye = (
        lax.broadcasted_iota(jnp.int32, (BLK, BLK), 0)
        == lax.broadcasted_iota(jnp.int32, (BLK, BLK), 1)
    )
    diagonal = jnp.where(eye, gram, 0.0)
    left = lax.rsqrt(jnp.sum(diagonal, axis=1, keepdims=True))
    top = lax.rsqrt(jnp.sum(diagonal, axis=0, keepdims=True))
    unit = gram * left * top
    g = [unit[tile * i : tile * i + tile, :] for i in range(count)]
    w = [jnp.where(lane_id == row_id + tile * i, 1.0, 0.0).astype(F32) for i in range(count)]

    def columns(t, base):
        return [jnp.broadcast_to(t[:, base + q : base + q + 1], (tile, BLK)) for q in range(tile)]

    def row(t, r):
        return jnp.broadcast_to(t[r : r + 1, :], (tile, BLK))

    def total(terms):
        while len(terms) > 1:
            terms = [terms[j] + terms[j + 1] for j in range(0, len(terms), 2)]
        return terms[0]

    for b in range(count):
        cols = columns(g[b], tile * b)
        pg, pw = g[b], w[b]
        inv = jnp.ones((tile, BLK), F32)
        for q in range(0, tile, 2):
            c0, c1 = cols[q], cols[q + 1]
            a00, a01, a11 = row(c0, q), row(c1, q), row(c1, q + 1)
            inv0 = 1.0 / a00
            inv_det = 1.0 / (a00 * a11 - a01 * a01)
            inv = jnp.where(row_id == q, inv0, jnp.where(row_id == q + 1, a00 * inv_det, inv))
            below = row_id > q + 1
            step0 = jnp.where(
                below, (c0 * a11 - c1 * a01) * inv_det, jnp.where(row_id == q + 1, a01 * inv0, 0.0)
            )
            step1 = jnp.where(below, (c1 * a00 - c0 * a01) * inv_det, 0.0)

            def reduce(t):
                return t - step0 * row(t, q) - step1 * row(t, q + 1)

            for m in range(q + 1, tile):
                cols[m] = reduce(cols[m])
            pg, pw = reduce(pg), reduce(pw)
        w[b] = pw * jnp.sqrt(inv)
        if b == count - 1:
            break
        zg, zw = pg * inv, pw * inv
        for q in range(tile - 1, 0, -1):
            back = jnp.where(row_id < q, cols[q] * inv, 0.0)
            zg, zw = zg - back * row(zg, q), zw - back * row(zw, q)
        rows_g = [row(zg, q) for q in range(tile)]
        rows_w = [row(zw, q) for q in range(tile)]
        for i in range(b + 1, count):
            cs = columns(g[i], tile * b)
            g[i] = g[i] - total([c * z for c, z in zip(cs, rows_g)])
            w[i] = w[i] - total([c * z for c, z in zip(cs, rows_w)])
    return jnp.concatenate(w, axis=0) * top


def first_sweep_kernel(tab, high, low, scale, x, mine, cross, x_new, full, near):
    x_new[...] = x[:, :BLK] - (mine[...] + cross[...]) * scale[...]
    apply_operator(high, low, x_new[...], full)
    pack_near(tab, full, near)


def second_sweep_kernel(
    tab, high, low, scale, x, mine, cross, first, x_new, full, near, *wide
):
    x_new[...] = x[:, BLK:] - (mine[...] + cross[...]) * scale[...]
    apply_operator(high, low, x_new[...], full)
    pack_near(tab, full, near)
    pack_wide(tab, (first, full), *wide)


def symmetric(g):
    return 0.5 * (g + g.T)


ROWS = ((0,), (0,))
LANES = ((1,), (1,))


def first_factor_kernel(tab, high, low, scale, x, mine, cross, *outs):
    x_new, product, inverse, scaled, near = outs
    x_new[...] = x[...] - (mine[...] + cross[...]) * scale[...]
    apply_operator(high, low, x_new[...], product)
    gram = symmetric(dot_full(x_new[...], product[...], ROWS))
    inverse[...] = inverse_factor(gram)
    scaled[...] = dot_split(product[...], inverse[...], LANES)
    pack_near(tab, scaled, near)


def second_product_kernel(
    high, low, scale, x, mine, cross, x0, product0, inverse0, x_out, product, lower, rest
):
    x_new = x[...] - (mine[...] + cross[...]) * scale[...]
    x_out[:, :BLK] = x0[...]
    x_out[:, BLK:] = x_new
    apply_operator(high, low, x_new, product)
    both = dot_full(x_new, jnp.concatenate([product0[...], product[...]], axis=1), ROWS)
    side = dot_full(both[:, :BLK], inverse0[...], LANES)
    lower[...] = side
    rest[...] = symmetric(both[:, BLK:]) - dot_full(side, side, LANES)


def second_factor_kernel(
    tab, product, lower, rest, scaled0, inverse, scaled, near, *wide
):
    inverse[...] = inverse_factor(rest[...])
    change = product[...] - dot_split(scaled0[...], lower[...], LANES)
    scaled[...] = dot_split(change, inverse[...], LANES)
    pack_near(tab, scaled, near)
    pack_wide(tab, (scaled0, scaled), *wide)


def basis_kernel(x, lower, inverse0, inverse, basis_high, basis_low):
    basis0 = dot_split(x[:, :BLK], inverse0[...], LANES)
    change = x[:, BLK:] - dot_split(basis0, lower[...], LANES)
    basis1 = dot_split(change, inverse[...], LANES)
    factor = math.sqrt(x.shape[0])
    for b in range(x.shape[0] // BLK):
        rows = slice(b * BLK, (b + 1) * BLK)
        for h, part in enumerate((basis0[rows], basis1[rows])):
            block_high, block_low = halves(factor * part.T)
            basis_high[b, h * BLK : (h + 1) * BLK, :] = block_high
            basis_low[b, h * BLK : (h + 1) * BLK, :] = block_low


def coupling_kernel(tab, basis_high, basis_low, *refs):
    received = (refs[:9], refs[9:18])
    out, stage, sem = refs[18:]
    core, wrapped = tab[OWN][CORE], tab[OWN][WRAPS]
    local = jnp.where(wrapped == 1, slot_of(-6, core), slot_of(2, core))

    def couple(place, slot, part):
        flag = flag_of(tab, OWN, slot)
        first, second = tab[OWN][2 * slot], tab[OWN][2 * slot + 1]
        left_high = jnp.concatenate([basis_high[first], basis_high[second]], axis=1)
        left_low = jnp.concatenate([basis_low[first], basis_low[second]], axis=1)
        for h in range(2):
            right = jnp.concatenate([part(h, 0), part(h, 1)], axis=0)
            right_high, right_low = halves(right)
            both = jnp.concatenate([right_high, right_low], axis=1)
            whole = dot(left_high, both)
            value = whole[:, :BLK] + whole[:, BLK:] + dot(left_low, right_high)
            stage[place, :, h * BLK : (h + 1) * BLK] = flag * value
        pltpu.make_async_copy(stage.at[place], out.at[slot], sem.at[place]).start()

    def at(index, place):
        start = 2 * place * BLK
        return lambda h, j: received[h][index][start + j * BLK : start + (j + 1) * BLK, :]

    def wide(index):
        return lambda h, j: received[h][index][(2 * h + j) * BLK : (2 * h + j + 1) * BLK, :]

    def from_ring(h, j):
        return received[h][0][rows_of(tab, SOURCE, local, j), :]

    slots = [
        (2 * REACH, wide(6)),
        (2 * REACH + 1, wide(7)),
        (slot_of(2, core), at(1, 0)),
        (slot_of(-6, core), wide(2)),
        (jnp.where(wrapped == 1, slot_of(6, core), slot_of(-2, core)), from_ring),
        (jnp.where(wrapped == 1, slot_of(-2, core), slot_of(6, core)), at(5, 0)),
        (slot_of(-4, core), at(3, 0)),
        (slot_of(4, core), at(4, 0)),
    ]
    for place, step in enumerate((1, -1, 3, -5, 5, -3)):
        slots.append((slot_of(step, core), at(8, place)))
    for place, (slot, part) in enumerate(slots):
        couple(place, slot, part)
    for place, (slot, part) in enumerate(slots):
        pltpu.make_async_copy(stage.at[place], out.at[slot], sem.at[place]).wait()


VMEM = pl.BlockSpec(memory_space=pltpu.VMEM)
SMEM = pl.BlockSpec(memory_space=pltpu.SMEM)
ANY = pl.BlockSpec(memory_space=pl.ANY)


def f32(*shape):
    return jax.ShapeDtypeStruct(shape, F32)


def b16(*shape):
    return jax.ShapeDtypeStruct(shape, BF16)


def call(kernel, outs, *args, scratch=(), out_specs=None):
    tables = 0
    body = kernel
    if isinstance(args[0], list):
        tables = len(args[0])
        args = (*args[0], *args[1:])

        def body(*refs):
            kernel(refs[:tables], *refs[tables:])

    return pl.pallas_call(
        body,
        out_shape=tuple(outs),
        in_specs=[SMEM] * tables + [VMEM] * (len(args) - tables),
        out_specs=tuple(out_specs or [VMEM] * len(outs)),
        scratch_shapes=list(scratch),
        compiler_params=pltpu.CompilerParams(vmem_limit_bytes=16 * 2**20),
        cost_estimate=pl.CostEstimate(flops=1, bytes_accessed=1, transcendentals=0),
    )(*args)


def on_device(local_operator, coarse_basis, neighbour_links, margin_blocks):
    matrix = local_operator[0, 0]
    initial = coarse_basis[0, 0]
    n, columns = initial.shape
    width = BLK
    assert columns == 2 * width
    place = lax.axis_index("sub")
    core = place % 2
    y = (place // 2) % RING
    wrapped = (y == jnp.where(core == 0, 0, RING - 1)).astype(jnp.int32)
    own = jnp.concatenate(
        [
            margin_blocks.reshape(2 * SLOTS),
            neighbour_links.reshape(2 * REACH),
            jnp.ones((2,), jnp.int32),
            jnp.stack([core, wrapped]),
        ]
    )
    tab = [own, send(own, route_core), send(own, route_ring)]

    full, pair = f32(n, width), f32(4 * BLK, width)
    square = f32(width, width)
    wide = [pair, pair, pair]

    def depart(up, down):
        return send_group(down, -1), send_group(up, 1)

    def forward(cut):
        ahead, back, layer = cut
        return send(ahead, route_ahead), send(back, route_back), send(layer, route_layer)

    def relay(ring0, ring1, near0, near1, far, hold):
        cut0 = call(relay_kernel, [pair, pair, pair], tab, ring0)
        if hold:
            ring1, near0, *cut0 = lax.optimization_barrier((ring1, near0, *cut0))
        cut1 = call(relay_kernel, [pair, pair, pair], tab, ring1)
        if hold:
            near1, far, *cut1 = lax.optimization_barrier((near1, far, *cut1))
        ring0, *cut1 = lax.optimization_barrier((ring0, *cut1))
        direct = send(near0, route_near), send(near1, route_near), send(far, route_far)
        return ring0, (forward(cut0), forward(cut1)), *direct

    def arrive(kernel, h, outs, block, ring, near, relayed, spread):
        ahead, back, layer = relayed
        far, above, below = spread
        parts = [ring, near, far, ahead, back, layer, above, below]
        theirs, *rest = call(functools.partial(kernel, h), outs, tab, block, *parts)
        return parts, rest, send(theirs, route_core)

    def summed(h, *moved):
        _, (mine,), theirs = arrive(cross_sum_kernel, h, [full, full], *moved)
        return mine, theirs

    def copied(h, *moved):
        parts, _, theirs = arrive(cross_copy_kernel, h, [f32(12 * BLK, width)], *moved)
        return parts + [theirs]

    high, low, scale, block0 = call(
        start_kernel, [b16(n, n), b16(n, n), full, full], matrix, initial
    )
    block0, *tab = lax.optimization_barrier((block0, *tab))
    ring0 = send(block0, route_ring)
    block1, near0, near1, *packets = call(
        next_kernel, [full, pair, pair, *wide], tab, high, low, initial, block0
    )
    ring1 = send(block1, route_ring)
    far, *packets = packets
    spread = depart(*packets)
    ring0, relayed, near0, near1, far = relay(
        ring0, ring1, near0, near1, far, True
    )
    spread = (far, *spread)
    sums0 = summed(0, block0, ring0, near0, relayed[0], spread)
    sums1 = summed(1, block1, ring1, near1, relayed[1], spread)

    x0, block0, near0 = call(
        first_sweep_kernel, [full, full, pair], tab, high, low, scale, initial, *sums0
    )
    ring0 = send(block0, route_ring)
    x1, block1, near1, *packets = call(
        second_sweep_kernel,
        [full, full, pair, *wide],
        tab,
        high,
        low,
        scale,
        initial,
        *sums1,
        block0,
    )
    ring1 = send(block1, route_ring)
    far, *packets = packets
    spread = depart(*packets)
    ring0, relayed, near0, near1, far = relay(
        ring0, ring1, near0, near1, far, True
    )
    spread = (far, *spread)
    sums0 = summed(0, block0, ring0, near0, relayed[0], spread)

    x0, product0, inverse0, scaled0, near0 = call(
        first_factor_kernel,
        [full, full, square, full, pair],
        tab,
        high,
        low,
        scale,
        x0,
        *sums0,
    )
    ring0 = send(scaled0, route_ring)
    ring1, scaled0 = lax.optimization_barrier((ring1, scaled0))
    sums1 = summed(1, block1, ring1, near1, relayed[1], spread)
    smoothed, product1, lower, rest = call(
        second_product_kernel,
        [f32(n, columns), full, square, square],
        high,
        low,
        scale,
        x1,
        *sums1,
        x0,
        product0,
        inverse0,
    )
    inverse1, scaled1, near1, *packets = call(
        second_factor_kernel,
        [square, full, pair, *wide],
        tab,
        product1,
        lower,
        rest,
        scaled0,
    )
    leaving1, ring0 = lax.optimization_barrier((scaled1, ring0))
    ring1 = send(leaving1, route_ring)
    far, *packets = packets
    spread = depart(*packets)
    turned = b16(n // BLK, columns, BLK)
    basis = call(basis_kernel, [turned, turned], smoothed, lower, inverse0, inverse1)
    ring0, relayed, near0, near1, far = relay(
        ring0, ring1, near0, near1, far, False
    )
    spread = (far, *spread)
    received0 = copied(0, scaled0, ring0, near0, relayed[0], spread)
    received1 = copied(1, scaled1, ring1, near1, relayed[1], spread)
    (coupling,) = call(
        coupling_kernel,
        [f32(SLOTS, columns, columns)],
        tab,
        *basis,
        *received0,
        *received1,
        scratch=[
            pltpu.VMEM((SLOTS, columns, columns), F32),
            pltpu.SemaphoreType.DMA((SLOTS,)),
        ],
        out_specs=[ANY],
    )
    return (smoothed[None, None], coupling[None, None])


def solution(mesh):
    in_specs = (
        P("sub", "grp", None, None),
        P("sub", "grp", None, None),
        P("sub", "grp", None),
        P("sub", "grp", None, None),
    )
    out_specs = (P("sub", "grp", None, None), P("sub", "grp", None, None, None))
    return jax.shard_map(
        on_device, mesh=mesh, in_specs=in_specs, out_specs=out_specs, check_vma=False
    )
```

```python
import functools
import math

import jax
import jax.numpy as jnp
from jax import lax
from jax.experimental import pallas as pl
from jax.experimental.pallas import tpu as pltpu
from jax.sharding import PartitionSpec as P

BLK = 128
REACH = 6
SLOTS = 2 * REACH + 2
RING = 4
OWN, OTHER, SOURCE = range(3)
CORE = 3 * SLOTS
WRAPS = CORE + 1
F32 = jnp.float32
BF16 = jnp.bfloat16


def sign(i):
    return 1 - 2 * (i % 2)


def along_ring(i, step):
    core, y, z = i % 2, (i // 2) % RING, i // (2 * RING)
    return (z * RING + (y + step) % RING) * 2 + core


def wraps(i):
    y = (i // 2) % RING
    return y == (0 if i % 2 == 0 else RING - 1)


def route_ring(i):
    return along_ring(i, sign(i))


def route_source(i):
    return along_ring(i, -sign(i))


def route_near(i):
    return i - 2 * sign(i)


def route_far(i):
    return i + 6 * sign(i)


def route_ahead(i):
    return route_source(i) + 4 * sign(i)


def route_back(i):
    return route_source(i) - 4 * sign(i)


def route_layer(i):
    return route_source(i) + (2 if wraps(i) else -6) * sign(i)


def route_core(i):
    return i ^ 1


def send(block, route):
    n = lax.axis_size("sub")
    return lax.ppermute(block, "sub", [(i, route(i) % n) for i in range(n)])


def send_group(block, distance):
    n = lax.axis_size("grp")
    return lax.ppermute(block, "grp", [(i, (i + distance) % n) for i in range(n)])


def slot_of(step, core):
    up = step - 1 if step > 0 else REACH - 1 - step
    down = REACH - 1 + step if step > 0 else -step - 1
    return jnp.where(core == 0, up, down)


def rows_of(tab, base, slot, j):
    return pl.ds(pl.multiple_of(tab[base][2 * slot + j] * BLK, BLK), BLK)


def flag_of(tab, base, slot):
    return tab[base][2 * SLOTS + slot].astype(F32)


def pick(tab, base, slot, source, target, place):
    for j in range(2):
        target[pl.ds((2 * place + j) * BLK, BLK), :] = source[rows_of(tab, base, slot, j), :]


def halves(x):
    high = x.astype(BF16)
    return high, (x - high.astype(F32)).astype(BF16)


def dot(a, b, dims=((1,), (0,))):
    return lax.dot_general(a, b, (dims, ((), ())), preferred_element_type=F32)


def dot_full(a, b, dims=((1,), (0,))):
    return lax.dot_general(
        a, b, (dims, ((), ())), precision=lax.Precision.HIGHEST, preferred_element_type=F32
    )


def dot_split(a, b, dims=((1,), (0,))):
    a_high, a_low = halves(a)
    b_high, b_low = halves(b)
    return dot(a_high, b_high, dims) + dot(a_high, b_low, dims) + dot(a_low, b_high, dims)


def apply_operator(high, low, x, out):
    x_high, x_low = halves(x)
    width = x.shape[1]
    both = jnp.concatenate([x_high, x_low], axis=1)
    step = 256
    for r in range(0, high.shape[0], step):
        first = dot(high[r : r + step, :], both)
        out[r : r + step, :] = (
            first[:, :width] + first[:, width:] + dot(low[r : r + step, :], x_high)
        )


def pack_near(tab, full, near):
    core = tab[OWN][CORE]
    pick(tab, OWN, slot_of(-2, core), full, near, 0)
    pick(tab, OWN, slot_of(-1, core), full, near, 1)


def pack_wide(tab, halves_of, far, up, down):
    core = tab[OWN][CORE]
    for h, full in enumerate(halves_of):
        pick(tab, OWN, slot_of(6, core), full, far, h)
        pick(tab, OWN, 2 * REACH, full, up, h)
        pick(tab, OWN, 2 * REACH + 1, full, down, h)


def start_kernel(a, x, high, low, scale, full):
    n = a.shape[0]
    step = 2 * BLK
    x_high, x_low = halves(x[:, :BLK])
    both = jnp.concatenate([x_high, x_low], axis=1)
    eye = (
        lax.broadcasted_iota(jnp.int32, (BLK, BLK), 0)
        == lax.broadcasted_iota(jnp.int32, (BLK, BLK), 1)
    )
    for r in range(0, n, step):
        row_high, row_low = halves(a[r : r + step, :])
        high[r : r + step, :] = row_high
        low[r : r + step, :] = row_low
        first = dot(row_high, both)
        full[r : r + step, :] = first[:, :BLK] + first[:, BLK:] + dot(row_low, x_high)
        for d in range(r, r + step, BLK):
            square = a[d : d + BLK, d : d + BLK]
            diagonal = jnp.sum(jnp.where(eye, square, 0.0), axis=1, keepdims=True)
            scale[d : d + BLK, :] = jnp.broadcast_to(0.5 / diagonal, (BLK, BLK))


def next_kernel(tab, high, low, x, first, full, near0, near1, *wide):
    pack_near(tab, first, near0)
    apply_operator(high, low, x[:, BLK:], full)
    pack_near(tab, full, near1)
    pack_wide(tab, (first, full), *wide)


def relay_kernel(tab, ring, ahead, back, layer):
    core, wrapped = tab[OWN][CORE], tab[OWN][WRAPS]
    pick(tab, SOURCE, slot_of(4, core), ring, ahead, 0)
    pick(tab, SOURCE, slot_of(5, core), ring, ahead, 1)
    pick(tab, SOURCE, slot_of(-4, core), ring, back, 0)
    pick(tab, SOURCE, slot_of(-3, core), ring, back, 1)
    mine = jnp.where(wrapped == 1, slot_of(2, core), slot_of(-6, core))
    theirs = jnp.where(wrapped == 1, slot_of(3, core), slot_of(-5, core))
    pick(tab, SOURCE, mine, ring, layer, 0)
    pick(tab, SOURCE, theirs, ring, layer, 1)


def add_rows(tab, base, slot, total, part):
    flag = flag_of(tab, base, slot)
    for j in range(2):
        rows = rows_of(tab, base, slot, j)
        total[rows, :] += flag * part(j)


def packet(ref, place):
    return lambda j: ref[pl.ds((2 * place + j) * BLK, BLK), :]


def block_rows(tab, base, slot, ref):
    return lambda j: ref[rows_of(tab, base, slot, j), :]


def cross_sum_kernel(h, tab, full, ring, near, far, ahead, back, layer, above, below, total, mine):
    core, wrapped = tab[OWN][CORE], tab[OWN][WRAPS]
    other = 1 - core
    total[...] = jnp.zeros(total.shape, F32)
    add = functools.partial(add_rows, tab, OTHER)
    add(slot_of(1, other), total, block_rows(tab, OWN, slot_of(1, core), full))
    add(slot_of(-1, other), total, packet(near, 1))
    here = jnp.where(wrapped == 1, slot_of(-5, core), slot_of(3, core))
    at = jnp.where(wrapped == 1, slot_of(-5, other), slot_of(3, other))
    add(at, total, block_rows(tab, SOURCE, here, ring))
    at = jnp.where(wrapped == 1, slot_of(3, other), slot_of(-5, other))
    add(at, total, packet(layer, 1))
    add(slot_of(5, other), total, packet(ahead, 1))
    add(slot_of(-3, other), total, packet(back, 1))
    mine[...] = full[...]
    add = functools.partial(add_rows, tab, OWN)
    add(slot_of(2, core), mine, packet(near, 0))
    add(slot_of(-6, core), mine, packet(far, h))
    here = jnp.where(wrapped == 1, slot_of(-6, core), slot_of(2, core))
    at = jnp.where(wrapped == 1, slot_of(6, core), slot_of(-2, core))
    add(at, mine, block_rows(tab, SOURCE, here, ring))
    at = jnp.where(wrapped == 1, slot_of(-2, core), slot_of(6, core))
    add(at, mine, packet(layer, 0))
    add(slot_of(-4, core), mine, packet(ahead, 0))
    add(slot_of(4, core), mine, packet(back, 0))
    add(2 * REACH, mine, packet(above, h))
    add(2 * REACH + 1, mine, packet(below, h))


def cross_copy_kernel(h, tab, full, ring, near, far, ahead, back, layer, above, below, out):
    core, wrapped = tab[OWN][CORE], tab[OWN][WRAPS]
    half = 2 * BLK
    pick(tab, OWN, slot_of(1, core), full, out, 0)
    out[half : 2 * half, :] = near[half:, :]
    here = jnp.where(wrapped == 1, slot_of(-5, core), slot_of(3, core))
    for j in range(2):
        local = ring[rows_of(tab, SOURCE, here, j), :]
        far = layer[half + j * BLK : half + (j + 1) * BLK, :]
        at = 2 * half + j * BLK
        out[at : at + BLK, :] = jnp.where(wrapped == 1, far, local)
        out[at + half : at + half + BLK, :] = jnp.where(wrapped == 1, local, far)
    out[4 * half : 5 * half, :] = ahead[half:, :]
    out[5 * half : 6 * half, :] = back[half:, :]


def inverse_factor(gram):
    tile = 8
    count = BLK // tile
    row_id = lax.broadcasted_iota(jnp.int32, (tile, BLK), 0)
    lane_id = lax.broadcasted_iota(jnp.int32, (tile, BLK), 1)
    eye = (
        lax.broadcasted_iota(jnp.int32, (BLK, BLK), 0)
        == lax.broadcasted_iota(jnp.int32, (BLK, BLK), 1)
    )
    diagonal = jnp.where(eye, gram, 0.0)
    left = lax.rsqrt(jnp.sum(diagonal, axis=1, keepdims=True))
    top = lax.rsqrt(jnp.sum(diagonal, axis=0, keepdims=True))
    unit = gram * left * top
    g = [unit[tile * i : tile * i + tile, :] for i in range(count)]
    w = [jnp.where(lane_id == row_id + tile * i, 1.0, 0.0).astype(F32) for i in range(count)]

    def columns(t, base):
        return [jnp.broadcast_to(t[:, base + q : base + q + 1], (tile, BLK)) for q in range(tile)]

    def row(t, r):
        return jnp.broadcast_to(t[r : r + 1, :], (tile, BLK))

    def total(terms):
        while len(terms) > 1:
            terms = [terms[j] + terms[j + 1] for j in range(0, len(terms), 2)]
        return terms[0]

    for b in range(count):
        cols = columns(g[b], tile * b)
        pg, pw = g[b], w[b]
        inv = jnp.ones((tile, BLK), F32)
        for q in range(0, tile, 2):
            c0, c1 = cols[q], cols[q + 1]
            a00, a01, a11 = row(c0, q), row(c1, q), row(c1, q + 1)
            inv0 = 1.0 / a00
            inv_det = 1.0 / (a00 * a11 - a01 * a01)
            inv = jnp.where(row_id == q, inv0, jnp.where(row_id == q + 1, a00 * inv_det, inv))
            below = row_id > q + 1
            step0 = jnp.where(
                below, (c0 * a11 - c1 * a01) * inv_det, jnp.where(row_id == q + 1, a01 * inv0, 0.0)
            )
            step1 = jnp.where(below, (c1 * a00 - c0 * a01) * inv_det, 0.0)

            def reduce(t):
                return t - step0 * row(t, q) - step1 * row(t, q + 1)

            for m in range(q + 1, tile):
                cols[m] = reduce(cols[m])
            pg, pw = reduce(pg), reduce(pw)
        w[b] = pw * jnp.sqrt(inv)
        if b == count - 1:
            break
        zg, zw = pg * inv, pw * inv
        for q in range(tile - 1, 0, -1):
            back = jnp.where(row_id < q, cols[q] * inv, 0.0)
            zg, zw = zg - back * row(zg, q), zw - back * row(zw, q)
        rows_g = [row(zg, q) for q in range(tile)]
        rows_w = [row(zw, q) for q in range(tile)]
        for i in range(b + 1, count):
            cs = columns(g[i], tile * b)
            g[i] = g[i] - total([c * z for c, z in zip(cs, rows_g)])
            w[i] = w[i] - total([c * z for c, z in zip(cs, rows_w)])
    return jnp.concatenate(w, axis=0) * top


def first_sweep_kernel(tab, high, low, scale, x, mine, cross, x_new, full, near):
    x_new[...] = x[:, :BLK] - (mine[...] + cross[...]) * scale[...]
    apply_operator(high, low, x_new[...], full)
    pack_near(tab, full, near)


def second_sweep_kernel(
    tab, high, low, scale, x, mine, cross, first, x_new, full, near, *wide
):
    x_new[...] = x[:, BLK:] - (mine[...] + cross[...]) * scale[...]
    apply_operator(high, low, x_new[...], full)
    pack_near(tab, full, near)
    pack_wide(tab, (first, full), *wide)


def symmetric(g):
    return 0.5 * (g + g.T)


ROWS = ((0,), (0,))
LANES = ((1,), (1,))


def first_factor_kernel(tab, high, low, scale, x, mine, cross, *outs):
    x_new, product, inverse, scaled, near = outs
    x_new[...] = x[...] - (mine[...] + cross[...]) * scale[...]
    apply_operator(high, low, x_new[...], product)
    gram = symmetric(dot_full(x_new[...], product[...], ROWS))
    inverse[...] = inverse_factor(gram)
    scaled[...] = dot_split(product[...], inverse[...], LANES)
    pack_near(tab, scaled, near)


def second_product_kernel(
    high, low, scale, x, mine, cross, x0, product0, inverse0, x_out, product, lower, rest
):
    x_new = x[...] - (mine[...] + cross[...]) * scale[...]
    x_out[:, :BLK] = x0[...]
    x_out[:, BLK:] = x_new
    apply_operator(high, low, x_new, product)
    both = dot_full(x_new, jnp.concatenate([product0[...], product[...]], axis=1), ROWS)
    side = dot_full(both[:, :BLK], inverse0[...], LANES)
    lower[...] = side
    rest[...] = symmetric(both[:, BLK:]) - dot_full(side, side, LANES)


def second_factor_kernel(
    tab, product, lower, rest, scaled0, inverse, scaled, near, *wide
):
    inverse[...] = inverse_factor(rest[...])
    change = product[...] - dot_split(scaled0[...], lower[...], LANES)
    scaled[...] = dot_split(change, inverse[...], LANES)
    pack_near(tab, scaled, near)
    pack_wide(tab, (scaled0, scaled), *wide)


def basis_kernel(x, lower, inverse0, inverse, basis_high, basis_low):
    basis0 = dot_split(x[:, :BLK], inverse0[...], LANES)
    change = x[:, BLK:] - dot_split(basis0, lower[...], LANES)
    basis1 = dot_split(change, inverse[...], LANES)
    factor = math.sqrt(x.shape[0])
    for b in range(x.shape[0] // BLK):
        rows = slice(b * BLK, (b + 1) * BLK)
        for h, part in enumerate((basis0[rows], basis1[rows])):
            block_high, block_low = halves(factor * part.T)
            basis_high[b, h * BLK : (h + 1) * BLK, :] = block_high
            basis_low[b, h * BLK : (h + 1) * BLK, :] = block_low


def coupling_kernel(tab, basis_high, basis_low, *refs):
    received = (refs[:9], refs[9:18])
    out, stage, sem = refs[18:]
    core, wrapped = tab[OWN][CORE], tab[OWN][WRAPS]
    local = jnp.where(wrapped == 1, slot_of(-6, core), slot_of(2, core))

    def couple(place, slot, part):
        flag = flag_of(tab, OWN, slot)
        first, second = tab[OWN][2 * slot], tab[OWN][2 * slot + 1]
        left_high = jnp.concatenate([basis_high[first], basis_high[second]], axis=1)
        left_low = jnp.concatenate([basis_low[first], basis_low[second]], axis=1)
        sides = [jnp.concatenate([part(h, 0), part(h, 1)], axis=0) for h in range(2)]
        right_high, right_low = halves(jnp.concatenate(sides, axis=1))
        value = dot(left_high, right_high) + dot(left_high, right_low) + dot(left_low, right_high)
        stage[place] = flag * value
        pltpu.make_async_copy(stage.at[place], out.at[slot], sem.at[place]).start()

    def at(index, place):
        start = 2 * place * BLK
        return lambda h, j: received[h][index][start + j * BLK : start + (j + 1) * BLK, :]

    def wide(index):
        return lambda h, j: received[h][index][(2 * h + j) * BLK : (2 * h + j + 1) * BLK, :]

    def from_ring(h, j):
        return received[h][0][rows_of(tab, SOURCE, local, j), :]

    slots = [
        (2 * REACH, wide(6)),
        (2 * REACH + 1, wide(7)),
        (slot_of(2, core), at(1, 0)),
        (slot_of(-6, core), wide(2)),
        (jnp.where(wrapped == 1, slot_of(6, core), slot_of(-2, core)), from_ring),
        (jnp.where(wrapped == 1, slot_of(-2, core), slot_of(6, core)), at(5, 0)),
        (slot_of(-4, core), at(3, 0)),
        (slot_of(4, core), at(4, 0)),
    ]
    for place, step in enumerate((1, -1, 3, -5, 5, -3)):
        slots.append((slot_of(step, core), at(8, place)))
    for place, (slot, part) in enumerate(slots):
        couple(place, slot, part)
    for place, (slot, part) in enumerate(slots):
        pltpu.make_async_copy(stage.at[place], out.at[slot], sem.at[place]).wait()


VMEM = pl.BlockSpec(memory_space=pltpu.VMEM)
SMEM = pl.BlockSpec(memory_space=pltpu.SMEM)
ANY = pl.BlockSpec(memory_space=pl.ANY)


def f32(*shape):
    return jax.ShapeDtypeStruct(shape, F32)


def b16(*shape):
    return jax.ShapeDtypeStruct(shape, BF16)


def call(kernel, outs, *args, scratch=(), out_specs=None):
    tables = 0
    body = kernel
    if isinstance(args[0], list):
        tables = len(args[0])
        args = (*args[0], *args[1:])

        def body(*refs):
            kernel(refs[:tables], *refs[tables:])

    return pl.pallas_call(
        body,
        out_shape=tuple(outs),
        in_specs=[SMEM] * tables + [VMEM] * (len(args) - tables),
        out_specs=tuple(out_specs or [VMEM] * len(outs)),
        scratch_shapes=list(scratch),
        compiler_params=pltpu.CompilerParams(vmem_limit_bytes=16 * 2**20),
        cost_estimate=pl.CostEstimate(flops=1, bytes_accessed=1, transcendentals=0),
    )(*args)


def on_device(local_operator, coarse_basis, neighbour_links, margin_blocks):
    matrix = local_operator[0, 0]
    initial = coarse_basis[0, 0]
    n, columns = initial.shape
    width = BLK
    assert columns == 2 * width
    place = lax.axis_index("sub")
    core = place % 2
    y = (place // 2) % RING
    wrapped = (y == jnp.where(core == 0, 0, RING - 1)).astype(jnp.int32)
    own = jnp.concatenate(
        [
            margin_blocks.reshape(2 * SLOTS),
            neighbour_links.reshape(2 * REACH),
            jnp.ones((2,), jnp.int32),
            jnp.stack([core, wrapped]),
        ]
    )
    tab = [own, send(own, route_core), send(own, route_ring)]

    full, pair = f32(n, width), f32(4 * BLK, width)
    square = f32(width, width)
    wide = [pair, pair, pair]

    def depart(up, down):
        return send_group(down, -1), send_group(up, 1)

    def forward(cut):
        ahead, back, layer = cut
        return send(ahead, route_ahead), send(back, route_back), send(layer, route_layer)

    def relay(ring0, ring1, near0, near1, far, hold):
        cut0 = call(relay_kernel, [pair, pair, pair], tab, ring0)
        if hold:
            ring1, near0, *cut0 = lax.optimization_barrier((ring1, near0, *cut0))
        cut1 = call(relay_kernel, [pair, pair, pair], tab, ring1)
        if hold:
            near1, far, *cut1 = lax.optimization_barrier((near1, far, *cut1))
        ring0, *cut1 = lax.optimization_barrier((ring0, *cut1))
        direct = send(near0, route_near), send(near1, route_near), send(far, route_far)
        return ring0, (forward(cut0), forward(cut1)), *direct

    def arrive(kernel, h, outs, block, ring, near, relayed, spread):
        ahead, back, layer = relayed
        far, above, below = spread
        parts = [ring, near, far, ahead, back, layer, above, below]
        theirs, *rest = call(functools.partial(kernel, h), outs, tab, block, *parts)
        return parts, rest, send(theirs, route_core)

    def summed(h, *moved):
        _, (mine,), theirs = arrive(cross_sum_kernel, h, [full, full], *moved)
        return mine, theirs

    def copied(h, *moved):
        parts, _, theirs = arrive(cross_copy_kernel, h, [f32(12 * BLK, width)], *moved)
        return parts + [theirs]

    high, low, scale, block0 = call(
        start_kernel, [b16(n, n), b16(n, n), full, full], matrix, initial
    )
    block0, *tab = lax.optimization_barrier((block0, *tab))
    ring0 = send(block0, route_ring)
    block1, near0, near1, *packets = call(
        next_kernel, [full, pair, pair, *wide], tab, high, low, initial, block0
    )
    ring1 = send(block1, route_ring)
    far, *packets = packets
    spread = depart(*packets)
    ring0, relayed, near0, near1, far = relay(
        ring0, ring1, near0, near1, far, True
    )
    spread = (far, *spread)
    sums0 = summed(0, block0, ring0, near0, relayed[0], spread)
    sums1 = summed(1, block1, ring1, near1, relayed[1], spread)

    x0, block0, near0 = call(
        first_sweep_kernel, [full, full, pair], tab, high, low, scale, initial, *sums0
    )
    ring0 = send(block0, route_ring)
    x1, block1, near1, *packets = call(
        second_sweep_kernel,
        [full, full, pair, *wide],
        tab,
        high,
        low,
        scale,
        initial,
        *sums1,
        block0,
    )
    ring1 = send(block1, route_ring)
    far, *packets = packets
    spread = depart(*packets)
    ring0, relayed, near0, near1, far = relay(
        ring0, ring1, near0, near1, far, True
    )
    spread = (far, *spread)
    sums0 = summed(0, block0, ring0, near0, relayed[0], spread)

    x0, product0, inverse0, scaled0, near0 = call(
        first_factor_kernel,
        [full, full, square, full, pair],
        tab,
        high,
        low,
        scale,
        x0,
        *sums0,
    )
    ring0 = send(scaled0, route_ring)
    ring1, scaled0 = lax.optimization_barrier((ring1, scaled0))
    sums1 = summed(1, block1, ring1, near1, relayed[1], spread)
    smoothed, product1, lower, rest = call(
        second_product_kernel,
        [f32(n, columns), full, square, square],
        high,
        low,
        scale,
        x1,
        *sums1,
        x0,
        product0,
        inverse0,
    )
    inverse1, scaled1, near1, *packets = call(
        second_factor_kernel,
        [square, full, pair, *wide],
        tab,
        product1,
        lower,
        rest,
        scaled0,
    )
    leaving1, ring0 = lax.optimization_barrier((scaled1, ring0))
    ring1 = send(leaving1, route_ring)
    far, *packets = packets
    spread = depart(*packets)
    turned = b16(n // BLK, columns, BLK)
    basis = call(basis_kernel, [turned, turned], smoothed, lower, inverse0, inverse1)
    ring0, relayed, near0, near1, far = relay(
        ring0, ring1, near0, near1, far, False
    )
    spread = (far, *spread)
    received0 = copied(0, scaled0, ring0, near0, relayed[0], spread)
    received1 = copied(1, scaled1, ring1, near1, relayed[1], spread)
    (coupling,) = call(
        coupling_kernel,
        [f32(SLOTS, columns, columns)],
        tab,
        *basis,
        *received0,
        *received1,
        scratch=[
            pltpu.VMEM((SLOTS, columns, columns), F32),
            pltpu.SemaphoreType.DMA((SLOTS,)),
        ],
        out_specs=[ANY],
    )
    return (smoothed[None, None], coupling[None, None])


def solution(mesh):
    in_specs = (
        P("sub", "grp", None, None),
        P("sub", "grp", None, None),
        P("sub", "grp", None),
        P("sub", "grp", None, None),
    )
    out_specs = (P("sub", "grp", None, None), P("sub", "grp", None, None, None))
    return jax.shard_map(
        on_device, mesh=mesh, in_specs=in_specs, out_specs=out_specs, check_vma=False
    )
```
